256 devices in a mesh: frame: 32 (over x, y, core), head: 8 (over z).
Axes of the slice: x: 4, y: 4, z: 8, core: 2. Of those that a mesh axis runs over, the one named last changes fastest.
Arguments:
- queries: bfloat16 [7168, 3072], P('frame', 'head'), may hold values from -24 to 24
- key_rows: bfloat16 [7168, 3072], P('frame', 'head'), may hold values from -24 to 24
- value_rows: bfloat16 [7168, 3072], P('frame', 'head'), may hold values from -5 to 5
- ref_keys: bfloat16 [32, 1024, 3072], P('frame', None, 'head'), may hold values from -5 to 5
- ref_values: bfloat16 [32, 1024, 3072], P('frame', None, 'head'), may hold values from -5 to 5
- key_lists: int32 [32, 8], P('frame'), may hold values from 0 to 31, as said below
- list_counts: int32 [32], P('frame'), may hold values from 1 to 8, as said below
- owner_index: int32 [1], replicated, may hold values from 0 to 31
- out_weight: bfloat16 [3072, 3072], P('head'), may hold values from -1.5 to 1.5
- residual: bfloat16 [7168, 3072], P('frame', 'head'), may hold values from -3 to 3
- gate_scale: float32 [3072], P('head'), may hold values from 0.5 to 2
Outputs:
- block_out: bfloat16 [7168, 3072], P('frame', 'head')
The draws below stay inside these ranges and needn't reach their ends.
Inputs may be any that keep to these rules, and one draw needn't show every extreme that they name: `key_lists`: the first list_counts[f] entries of row f are distinct frames other than f, each within 4 frames of f; the remaining entries equal f. `list_counts`: some frame lists every frame within 4 of it.
All inputs are finite; a program needn't handle non-finite values.
Results may differ from the reference program's by a relative error of at most 0.02.
Values may be sent and summed in bfloat16 or wider, within the bound.
A program may use at most 64 MiB of HBM per device.

```python
import math
import jax
import jax.numpy as jnp
from jax import lax

D = 3072
HEADS = 24
HD = 128
TQ = 224
REF = 1024
REACH = 4
MAXL = 8
FRAMES = 32
TOKENS = 7168


def paired_rows(key):
    folded = jax.random.fold_in(key, 7)
    key_one, key_two = jax.random.split(folded)
    query_draw = jnp.clip(jax.random.normal(key_one, (TOKENS, D), jnp.float32), -4.0, 4.0)
    key_draw = jnp.clip(jax.random.normal(key_two, (TOKENS, D), jnp.float32), -4.0, 4.0)
    return (query_draw, key_draw)


def draw_queries(key, part):
    return paired_rows(key)[0].astype(jnp.bfloat16)


def draw_key_rows(key, part):
    return paired_rows(key)[1].astype(jnp.bfloat16)


def frame_lists(key):
    folded = jax.random.fold_in(key, 11)
    key_one, key_two, key_three = jax.random.split(folded, 3)
    frame_ids = jnp.arange(FRAMES, dtype=jnp.int32)[:, None]
    offsets = jnp.concatenate([jnp.arange(-REACH, 0, dtype=jnp.int32), jnp.arange(1, REACH + 1, dtype=jnp.int32)])
    candidates = frame_ids + offsets[None, :]
    inside = (candidates >= 0) & (candidates < FRAMES)
    available = jnp.sum(inside.astype(jnp.int32), axis=1)
    priority = jax.random.randint(key_one, (FRAMES, MAXL), 0, 1 << 20, dtype=jnp.int32) * MAXL + jnp.arange(MAXL, dtype=jnp.int32)[None, :]
    priority = jnp.where(inside, priority, -1)
    ranking = jnp.argsort(-priority, axis=1, stable=True)
    ordered = jnp.take_along_axis(candidates, ranking, axis=1)
    counts = jnp.minimum(jax.random.randint(key_two, (FRAMES,), 1, MAXL + 1, dtype=jnp.int32), available)
    full_frame = jnp.minimum(REACH + jax.random.randint(key_three, (), 0, max(FRAMES - 2 * REACH, 1), dtype=jnp.int32), FRAMES - 1)
    counts = jnp.where(frame_ids[:, 0] == full_frame, available, counts)
    slot_ids = jnp.arange(MAXL, dtype=jnp.int32)
    listed = jnp.where(slot_ids[None, :] < counts[:, None], ordered, frame_ids)
    return (listed.astype(jnp.int32), counts.astype(jnp.int32))


def draw_key_lists(key, part):
    return frame_lists(key)[0]


def draw_list_counts(key, part):
    return frame_lists(key)[1]


def block_levels(key, shape, cuts, low, high):
    loudness = 1.0
    for axis_at, blocks in cuts:
        steps = jax.random.uniform(jax.random.fold_in(jax.random.fold_in(key, 6), axis_at), (blocks,), jnp.float32, low / len(cuts), high / len(cuts))
        loudness = loudness * jnp.repeat(jnp.exp(steps), shape[axis_at] // blocks).reshape((-1,) + (1,) * (len(shape) - 1 - axis_at))
    return loudness


def centred(own_key, dims, scale, reach, cuts=(), kind=jnp.bfloat16):
    values = scale * jax.random.normal(own_key, dims, jnp.float32)
    if cuts:
        values = values * block_levels(own_key, dims, cuts, -0.22, 0.18)
    return jnp.clip(values, -reach, reach).astype(kind)


def setup_inputs(seed: int = 0) -> dict:
    splits = jax.random.split(jax.random.key(seed), 12)
    queries = draw_queries(jax.random.fold_in(splits[11], 71), 0)
    key_rows = draw_key_rows(jax.random.fold_in(splits[11], 71), 0)
    value_rows = centred(splits[2], (TOKENS, D), 1.0, 5.0, ((0, 32), (1, 8)))
    ref_keys = centred(splits[3], (FRAMES, REF, D), 1.0, 5.0, ((0, 32), (2, 8)))
    ref_values = centred(splits[4], (FRAMES, REF, D), 1.0, 5.0, ((0, 32), (2, 8)))
    key_lists = draw_key_lists(jax.random.fold_in(splits[11], 71), 0)
    list_counts = draw_list_counts(jax.random.fold_in(splits[11], 71), 0)
    owner_index = jax.random.randint(splits[7], (1,), 0, FRAMES).astype(jnp.int32)
    out_weight = centred(splits[8], (D, D), 0.25, 1.5, ((0, 8),))
    residual = centred(splits[9], (TOKENS, D), 0.5, 3.0, ((0, 32), (1, 8)))
    gate_scale = jnp.clip(jnp.exp(math.log(2.0) - 1.3862944 * jax.random.uniform(splits[10], (D,), jnp.float32) ** block_levels(splits[10], (D,), ((0, 8),), -0.2, 0.2)), 0.5, 2.0)
    return dict(queries=queries, key_rows=key_rows, value_rows=value_rows, ref_keys=ref_keys, ref_values=ref_values, key_lists=key_lists, list_counts=list_counts, owner_index=owner_index, out_weight=out_weight, residual=residual, gate_scale=gate_scale)


def reference(queries, key_rows, value_rows, ref_keys, ref_values, key_lists, list_counts, owner_index, out_weight, residual, gate_scale):
    inv_root = 1.0 / math.sqrt(HD)
    style_keys = lax.dynamic_index_in_dim(ref_keys, owner_index[0], 0, keepdims=False).astype(jnp.float32).reshape(REF, HEADS, HD)
    style_values = lax.dynamic_index_in_dim(ref_values, owner_index[0], 0, keepdims=False).astype(jnp.float32).reshape(REF, HEADS, HD)
    key_frames = key_rows.reshape(FRAMES, TQ, HEADS, HD)
    value_frames = value_rows.reshape(FRAMES, TQ, HEADS, HD)
    query_frames = queries.reshape(FRAMES, TQ, HEADS, HD)

    def attend_frame(frame_id):
        chosen = jnp.concatenate([frame_id[None].astype(jnp.int32), key_lists[frame_id].astype(jnp.int32)])
        slot_live = jnp.concatenate([jnp.ones((1,), bool), jnp.arange(MAXL, dtype=jnp.int32) < list_counts[frame_id]])
        near_keys = key_frames[chosen].astype(jnp.float32).reshape((MAXL + 1) * TQ, HEADS, HD)
        near_values = value_frames[chosen].astype(jnp.float32).reshape((MAXL + 1) * TQ, HEADS, HD)
        all_keys = jnp.concatenate([style_keys, near_keys], axis=0)
        all_values = jnp.concatenate([style_values, near_values], axis=0)
        allowed = jnp.concatenate([jnp.ones((REF,), bool), jnp.repeat(slot_live, TQ)])
        query_heads = query_frames[frame_id].astype(jnp.float32)
        scores = jnp.einsum('qhd,khd->hqk', query_heads, all_keys) * inv_root
        scores = jnp.where(allowed[None, None, :], scores, -jnp.inf)
        row_max = lax.optimization_barrier(jnp.max(scores, axis=-1, keepdims=True))
        weights = jnp.exp(scores - row_max)
        row_total = lax.optimization_barrier(jnp.sum(weights, axis=-1))
        rounded = lax.optimization_barrier(weights.astype(jnp.bfloat16)).astype(jnp.float32)
        combined = jnp.einsum('hqk,khd->qhd', rounded, all_values) / row_total.T[:, :, None]
        return combined.astype(jnp.bfloat16).reshape(TQ, D)
    attended = lax.map(attend_frame, jnp.arange(FRAMES, dtype=jnp.int32)).reshape(TOKENS, D)
    projected = jnp.dot(attended, out_weight, preferred_element_type=jnp.float32)
    return (residual.astype(jnp.float32) + gate_scale[None, :] * projected).astype(jnp.bfloat16)
```

```python
import math

import jax
import jax.numpy as jnp
from jax import lax
from jax.experimental import pallas as pl
from jax.experimental.pallas import tpu as pltpu
from jax.sharding import PartitionSpec as P

HD = 128
REACH = 4
MESH = pl.DeviceIdType.MESH
SCALE = math.log2(math.e) / math.sqrt(HD)
FAR = 1e30
LANES = 128


def dot(a, b, dims):
    return lax.dot_general(a, b, (dims, ((), ())), preferred_element_type=jnp.float32)


def kernel(
    q_hbm, k_hbm, v_hbm, rk_hbm, rv_hbm, lists, counts, owner, w_hbm, res_hbm, gate_ref,
    out_ref,
    q_buf, k_near, v_near, ref_own, ref_sib, ref_sel, x_parts, x_sum, y_parts, style,
    w_buf, res_buf, top, total, acc, att, z_out, z_in, local_sem, send_sem, recv_sem, z_send, z_recv,
):
    rows, width = q_buf.shape
    heads = width // HD
    slots = lists.shape[1]
    ref_rows = style.shape[1]
    quarter, piece = ref_rows // 4, ref_rows // 16
    half = rows // 2

    frame = lax.axis_index("frame")
    z = lax.axis_index("head")
    core = lax.rem(frame, 2)
    chip = frame // 2
    x, y = chip // 4, lax.rem(chip, 4)
    sibling = (frame + 1 - 2 * core, z)

    def at_x(j):
        return (lax.rem(x + j, 4) * 8 + y * 2 + core, z)

    def at_y(j):
        return (x * 8 + lax.rem(y + j, 4) * 2 + core, z)

    def at_chip(o):
        return (lax.rem(chip + o + 16, 16) * 2 + core, z)

    def at_z(o):
        return (frame, lax.rem(z + o + 8, 8))

    made = []

    def send(src, dst, device):
        i = len(made)
        copy = pltpu.make_async_remote_copy(
            src_ref=src, dst_ref=dst, send_sem=send_sem.at[i], recv_sem=recv_sem.at[i],
            device_id=device, device_id_type=MESH,
        )
        copy.start()
        made.append(copy)
        return copy

    def fetch(src, dst, i):
        copy = pltpu.make_async_copy(src, dst, local_sem.at[i])
        copy.start()
        return copy

    own = 4 + core
    get_q = fetch(q_hbm, q_buf, 0)
    get_k = fetch(k_hbm, k_near.at[own], 1)
    get_v = fetch(v_hbm, v_near.at[own], 2)

    @pl.when(core == 0)
    def _():
        pltpu.make_async_copy(rk_hbm.at[0], ref_own, local_sem.at[3]).start()

    @pl.when(core == 1)
    def _():
        pltpu.make_async_copy(rv_hbm.at[0], ref_own, local_sem.at[3]).start()

    get_w = fetch(w_hbm, w_buf, 4)
    get_res = fetch(res_hbm, res_buf, 5)

    barrier = pltpu.get_barrier_semaphore()
    partners = (
        [sibling]
        + [at_x(j) for j in (1, 2, 3)]
        + [at_y(j) for j in (1, 2, 3)]
        + [at_chip(o) for o in (1, -1, 2, -2)]
        + [at_z(1), at_z(-1)]
    )
    for device in partners:
        pl.semaphore_signal(barrier, inc=1, device_id=device, device_id_type=MESH)
    pl.semaphore_wait(barrier, len(partners))

    swap = pltpu.make_async_remote_copy(
        src_ref=rv_hbm.at[0], dst_ref=ref_sib, send_sem=send_sem.at[0], recv_sem=recv_sem.at[0],
        device_id=sibling, device_id_type=MESH,
    )
    made.append(swap)
    pl.when(core == 0)(swap.start)

    @pl.when(core == 1)
    def _():
        pltpu.make_async_remote_copy(
            src_ref=rk_hbm.at[0], dst_ref=ref_sib, send_sem=send_sem.at[0], recv_sem=recv_sem.at[0],
            device_id=sibling, device_id_type=MESH,
        ).start()

    to_sib = [send(k_hbm, k_near.at[own], sibling), send(v_hbm, v_near.at[own], sibling)]

    def to_chip(o):
        slot = (2 - o) * 2 + core
        return [send(k_hbm, k_near.at[slot], at_chip(o)), send(v_hbm, v_near.at[slot], at_chip(o))]

    near = {o: to_chip(o) for o in (1, -1)}

    top[...] = jnp.full(top.shape, -FAR, jnp.float32)
    total[...] = jnp.zeros(total.shape, jnp.float32)
    acc[...] = jnp.zeros(acc.shape, jnp.float32)

    def absorb(k_ref, v_ref, penalty):
        for h in range(heads):
            cols = pl.ds(h * HD, HD)
            scores = dot(k_ref[:, cols], q_buf[:, cols], ((1,), (1,)))
            best = jnp.max(scores, axis=0, keepdims=True)
            if penalty is not None:
                best = best - penalty
            before = top[h]
            after = jnp.maximum(before, best)
            factor = jnp.exp2((before - after) * SCALE)
            shift = after * SCALE
            if penalty is not None:
                shift = shift + penalty
            weights = jnp.exp2(scores * SCALE - shift)
            top[h] = after
            total[h] = total[h] * factor + jnp.sum(weights, axis=0, keepdims=True)
            acc[h] = acc[h] * factor + dot(v_ref[:, cols], weights.astype(jnp.bfloat16), ((0,), (0,)))

    def absorb_near(slot):
        there = frame - core - 4 + slot
        hits = jnp.int32(0)
        for j in range(slots):
            hits += jnp.where((lists[0, j] == there) & (j < counts[0]), 1, 0)
        penalty = jnp.where(hits > 0, jnp.float32(0), jnp.float32(FAR))
        absorb(k_near.at[slot], v_near.at[slot], penalty)

    def absorb_two(slot_a, slot_b):
        def body(i, carry):
            absorb_near(slot_a + i * (slot_b - slot_a))
            return carry

        lax.fori_loop(0, 2, body, 0)

    get_q.wait()
    get_k.wait()
    get_v.wait()
    absorb(k_near.at[own], v_near.at[own], None)

    pltpu.make_async_copy(rk_hbm.at[0], ref_own, local_sem.at[3]).wait()
    swap.wait_recv()
    mine = jnp.where(owner[0] == frame, 1.0, 0.0).astype(jnp.bfloat16)
    theirs = jnp.where(owner[0] == frame + 1 - 2 * core, 1.0, 0.0).astype(jnp.bfloat16)
    ref_sel[...] = ref_own[...] * mine + ref_sib[...] * theirs

    def q_rows(j):
        return pl.ds(pl.multiple_of(lax.rem(x + j, 4) * quarter, quarter), quarter)

    rsx = [send(ref_sel.at[q_rows(j)], x_parts.at[j - 1], at_x(j)) for j in (1, 3, 2)]
    near.update({o: to_chip(o) for o in (2, -2)})

    for copy in to_sib:
        copy.wait_recv()
    absorb_near(5 - core)

    passed = []

    def pass_on(slot):
        return [send(k_near.at[slot], k_near.at[slot], sibling), send(v_near.at[slot], v_near.at[slot], sibling)]

    for o in (1, -1):
        for copy in near[o]:
            copy.wait_recv()
        passed += pass_on((2 - o) * 2 + core)
    absorb_two(2 + core, 6 + core)

    for copy in rsx:
        copy.wait_recv()
    x_sum[...] = ref_sel[q_rows(0)] + x_parts[0] + x_parts[1] + x_parts[2]

    def p_rows(j):
        return pl.ds(pl.multiple_of(lax.rem(y + j, 4) * piece, piece), piece)

    rsy = [send(x_sum.at[p_rows(j)], y_parts.at[j - 1], at_y(j)) for j in (1, 3, 2)]

    for copy in passed:
        copy.wait_recv()
    absorb_two(3 - core, 7 - core)

    for copy in rsy:
        copy.wait_recv()
    my_piece = pl.ds(pl.multiple_of(x * quarter + y * piece, piece), piece)
    carried = style.at[core]
    carried[my_piece] = x_sum[p_rows(0)] + y_parts[0] + y_parts[1] + y_parts[2]
    agy = [send(carried.at[my_piece], carried.at[my_piece], at_y(j)) for j in (1, 3, 2)]

    for o in (2, -2):
        for copy in near[o]:
            copy.wait_recv()
    last = pass_on(8 - 7 * core)
    absorb_two(core, 8 + core)

    for copy in agy:
        copy.wait_recv()
    agx = {j: send(carried.at[q_rows(0)], carried.at[q_rows(0)], at_x(j)) for j in (1, 3, 2)}
    shown = send(carried.at[q_rows(0)], carried.at[q_rows(0)], sibling)

    for copy in last:
        copy.wait_recv()
    absorb_near(1 + 7 * core)

    shown.wait_recv()

    def absorb_style(j):
        absorb(style.at[0, q_rows(j)], style.at[1, q_rows(j)], None)

    absorb_style(0)
    for j in (1, 3, 2):
        agx[j].wait_recv()
        there = q_rows(4 - j)
        shown = send(carried.at[there], carried.at[there], sibling)
        shown.wait_recv()
        absorb_style(4 - j)

    for h in range(heads):
        att[:, pl.ds(h * HD, HD)] = (acc[h] / total[h]).T.astype(jnp.bfloat16)

    get_w.wait()
    parts = width // LANES

    def share(way, step):
        chunk = lax.rem(z - 1 - step + 16, 8) if way == 0 else lax.rem(z + 1 + step, 8)
        cols = pl.ds(pl.multiple_of(chunk * width, LANES), width)
        return dot(att[pl.ds(way * half, half), :], w_buf[:, cols], ((1,), (0,)))

    def hop(way, step, part):
        i = (step * 2 + way) * parts + part
        return pltpu.make_async_remote_copy(
            src_ref=z_out.at[step, way, part], dst_ref=z_in.at[step, way, part],
            send_sem=z_send.at[i], recv_sem=z_recv.at[i],
            device_id=at_z(1 if way == 0 else -1), device_id_type=MESH,
        )

    def ring(step, first):
        shares = [share(way, step) for way in (0, 1)]
        for part in range(parts):
            for way in (0, 1):
                value = shares[way][:, part * LANES : (part + 1) * LANES]
                if not first:
                    hop(way, step - 1, part).wait_recv()
                    value = value + z_in[step - 1, way, part].astype(jnp.float32)
                z_out[step, way, part] = value.astype(jnp.bfloat16)
                hop(way, step, part).start()

    ring(0, True)

    def body(step, carry):
        ring(step, False)
        return carry

    lax.fori_loop(1, 7, body, 0)
    get_res.wait()
    shares = [share(way, 7) for way in (0, 1)]
    for part in range(parts):
        for way in (0, 1):
            hop(way, 6, part).wait_recv()
            cols = pl.ds(part * LANES, LANES)
            some = pl.ds(way * half, half)
            value = shares[way][:, part * LANES : (part + 1) * LANES] + z_in[6, way, part].astype(jnp.float32)
            out_ref[some, cols] = (
                res_buf[some, cols].astype(jnp.float32) + gate_ref[:, cols] * value
            ).astype(jnp.bfloat16)

    for copy in made:
        copy.wait_send()

    def drain(step, carry):
        for way in (0, 1):
            for part in range(parts):
                hop(way, step, part).wait_send()
        return carry

    lax.fori_loop(0, 7, drain, 0)


def per_device(
    queries, key_rows, value_rows, ref_keys, ref_values, key_lists, list_counts, owner_index, out_weight, residual,
    gate_scale,
):
    rows, width = queries.shape
    heads = width // HD
    ref_rows = ref_keys.shape[1]
    quarter, piece = ref_rows // 4, ref_rows // 16
    bf16, f32 = jnp.bfloat16, jnp.float32
    hbm = pl.BlockSpec(memory_space=pl.ANY)
    vmem = pl.BlockSpec(memory_space=pltpu.VMEM)
    smem = pl.BlockSpec(memory_space=pltpu.SMEM)
    copies = 40
    hops = 7 * 2 * (width // LANES)
    return pl.pallas_call(
        kernel,
        out_shape=jax.ShapeDtypeStruct((rows, width), bf16),
        in_specs=[hbm] * 5 + [smem] * 3 + [hbm, hbm, vmem],
        out_specs=vmem,
        scratch_shapes=[
            pltpu.VMEM((rows, width), bf16),
            pltpu.VMEM((10, rows, width), bf16),
            pltpu.VMEM((10, rows, width), bf16),
            pltpu.VMEM((ref_rows, width), bf16),
            pltpu.VMEM((ref_rows, width), bf16),
            pltpu.VMEM((ref_rows, width), bf16),
            pltpu.VMEM((3, quarter, width), bf16),
            pltpu.VMEM((quarter, width), bf16),
            pltpu.VMEM((3, piece, width), bf16),
            pltpu.VMEM((2, ref_rows, width), bf16),
            pltpu.VMEM(out_weight.shape, bf16),
            pltpu.VMEM((rows, width), bf16),
            pltpu.VMEM((heads, 1, rows), f32),
            pltpu.VMEM((heads, 1, rows), f32),
            pltpu.VMEM((heads, HD, rows), f32),
            pltpu.VMEM((rows, width), bf16),
            pltpu.VMEM((7, 2, width // LANES, rows // 2, LANES), bf16),
            pltpu.VMEM((7, 2, width // LANES, rows // 2, LANES), bf16),
            pltpu.SemaphoreType.DMA((6,)),
            pltpu.SemaphoreType.DMA((copies,)),
            pltpu.SemaphoreType.DMA((copies,)),
            pltpu.SemaphoreType.DMA((hops,)),
            pltpu.SemaphoreType.DMA((hops,)),
        ],
        compiler_params=pltpu.CompilerParams(
            collective_id=0, has_side_effects=True, vmem_limit_bytes=48 * 1024 * 1024
        ),
        name="block",
    )(
        queries, key_rows, value_rows, ref_keys, ref_values, key_lists, list_counts, owner_index, out_weight,
        residual, gate_scale.reshape(1, width),
    )


def solution(mesh):
    placed = (
        P("frame", "head"),
        P("frame", "head"),
        P("frame", "head"),
        P("frame", None, "head"),
        P("frame", None, "head"),
        P("frame", None),
        P("frame"),
        P(),
        P("head", None),
        P("frame", "head"),
        P("head"),
    )
    return jax.shard_map(
        per_device, mesh=mesh, in_specs=placed, out_specs=P("frame", "head"), check_vma=False
    )
```

```python
import math

import jax
import jax.numpy as jnp
from jax import lax
from jax.experimental import pallas as pl
from jax.experimental.pallas import tpu as pltpu
from jax.sharding import PartitionSpec as P

HD = 128
REACH = 4
MESH = pl.DeviceIdType.MESH
SCALE = math.log2(math.e) / math.sqrt(HD)
FAR = 1e30
LANES = 128


def dot(a, b, dims):
    return lax.dot_general(a, b, (dims, ((), ())), preferred_element_type=jnp.float32)


def kernel(
    q_hbm, k_hbm, v_hbm, rk_hbm, rv_hbm, lists, counts, owner, w_hbm, res_hbm, gate_ref,
    out_ref,
    q_buf, k_near, v_near, ref_own, ref_sib, ref_sel, x_parts, x_sum, y_parts, style,
    w_buf, res_buf, top, total, acc, att, z_out, z_in, local_sem, send_sem, recv_sem, z_send, z_recv,
):
    rows, width = q_buf.shape
    heads = width // HD
    slots = lists.shape[1]
    ref_rows = style.shape[1]
    half = rows // 2

    frame = lax.axis_index("frame")
    z = lax.axis_index("head")
    core = lax.rem(frame, 2)
    chip = frame // 2
    x, y = chip // 4, lax.rem(chip, 4)
    sibling = (frame + 1 - 2 * core, z)

    def at_x(j):
        return (lax.rem(x + j, 4) * 8 + y * 2 + core, z)

    def at_y(j):
        return (x * 8 + lax.rem(y + j, 4) * 2 + core, z)

    def at_chip(o):
        return (lax.rem(chip + o + 16, 16) * 2 + core, z)

    def at_z(o):
        return (frame, lax.rem(z + o + 8, 8))

    made = []

    def send(src, dst, device):
        i = len(made)
        copy = pltpu.make_async_remote_copy(
            src_ref=src, dst_ref=dst, send_sem=send_sem.at[i], recv_sem=recv_sem.at[i],
            device_id=device, device_id_type=MESH,
        )
        copy.start()
        made.append(copy)
        return copy

    def fetch(src, dst, i):
        copy = pltpu.make_async_copy(src, dst, local_sem.at[i])
        copy.start()
        return copy

    own = 4 + core
    block, bit = ref_rows // 8, ref_rows // 32
    get_q = fetch(q_hbm, q_buf, 0)
    get_k = fetch(k_hbm, k_near.at[own], 1)
    get_v = fetch(v_hbm, v_near.at[own], 2)

    style_in = ((rk_hbm, rv_hbm), (rv_hbm, rk_hbm))

    def keep(s, which):
        rows_of = pl.ds(s * 4 * block, 4 * block)
        return pltpu.make_async_copy(style_in[which][0].at[0, rows_of], ref_own.at[rows_of], local_sem.at[3 + s])

    def give(s, which):
        rows_of = pl.ds(s * 4 * block, 4 * block)
        return pltpu.make_async_remote_copy(
            src_ref=style_in[which][1].at[0, rows_of], dst_ref=ref_sib.at[rows_of],
            send_sem=send_sem.at[s], recv_sem=recv_sem.at[s], device_id=sibling, device_id_type=MESH,
        )

    for which in (0, 1):

        @pl.when(core == which)
        def _():
            for s in (0, 1):
                keep(s, which).start()

    get_w = fetch(w_hbm, w_buf, 5)
    get_res = fetch(res_hbm, res_buf, 6)

    barrier = pltpu.get_barrier_semaphore()
    partners = (
        [sibling]
        + [at_x(j) for j in (1, 2, 3)]
        + [at_y(j) for j in (1, 2, 3)]
        + [at_chip(o) for o in (1, -1)]
        + [at_z(1), at_z(-1)]
    )
    for device in partners:
        pl.semaphore_signal(barrier, inc=1, device_id=device, device_id_type=MESH)
    pl.semaphore_wait(barrier, len(partners))

    for which in (0, 1):

        @pl.when(core == which)
        def _():
            for s in (0, 1):
                give(s, which).start()

    made += [give(s, 0) for s in (0, 1)]

    to_sib = [send(k_hbm, k_near.at[own], sibling), send(v_hbm, v_near.at[own], sibling)]

    def slot_of(o):
        return (o + 2) * 2 + core

    near = {(o, 0): send(k_hbm, k_near.at[slot_of(-o)], at_chip(o)) for o in (1, -1)}

    top[...] = jnp.full(top.shape, -FAR, jnp.float32)
    total[...] = jnp.zeros(total.shape, jnp.float32)
    acc[...] = jnp.zeros(acc.shape, jnp.float32)

    def absorb(k_ref, v_ref, penalty):
        for h in range(heads):
            cols = pl.ds(h * HD, HD)
            scores = dot(k_ref[:, cols], q_buf[:, cols], ((1,), (1,)))
            best = jnp.max(scores, axis=0, keepdims=True)
            if penalty is not None:
                best = best - penalty
            before = top[h]
            after = jnp.maximum(before, best)
            factor = jnp.exp2((before - after) * SCALE)
            shift = after * SCALE
            if penalty is not None:
                shift = shift + penalty
            weights = jnp.exp2(scores * SCALE - shift)
            top[h] = after
            total[h] = total[h] * factor + jnp.sum(weights, axis=0, keepdims=True)
            acc[h] = acc[h] * factor + dot(v_ref[:, cols], weights.astype(jnp.bfloat16), ((0,), (0,)))

    def absorb_near(slot):
        there = frame - core - 4 + slot
        hits = jnp.int32(0)
        for j in range(slots):
            hits += jnp.where((lists[0, j] == there) & (j < counts[0]), 1, 0)
        penalty = jnp.where(hits > 0, jnp.float32(0), jnp.float32(FAR))
        absorb(k_near.at[slot], v_near.at[slot], penalty)

    def absorb_two(slot_a, slot_b):
        def body(i, carry):
            absorb_near(slot_a + i * (slot_b - slot_a))
            return carry

        lax.fori_loop(0, 2, body, 0)

    first_axis, first_at, second_axis, second_at = (x, y), (at_x, at_y), (y, x), (at_y, at_x)
    order = (1, 3, 2)
    mine = jnp.where(owner[0] == frame, 1.0, 0.0).astype(jnp.bfloat16)
    theirs = jnp.where(owner[0] == frame + 1 - 2 * core, 1.0, 0.0).astype(jnp.bfloat16)
    carried = style.at[core]

    def block_rows(s, j):
        return pl.ds(pl.multiple_of(s * 4 * block + lax.rem(first_axis[s] + j, 4) * block, block), block)

    def bit_rows(s, j):
        return pl.ds(pl.multiple_of(lax.rem(second_axis[s] + j, 4) * bit, bit), bit)

    def own_bit(s):
        return pl.ds(
            pl.multiple_of(s * 4 * block + first_axis[s] * block + second_axis[s] * bit, bit), bit
        )

    def choose(s):
        rows_of = pl.ds(s * 4 * block, 4 * block)
        keep(s, 0).wait()
        made[s].wait_recv()
        ref_sel[rows_of] = ref_own[rows_of] * mine + ref_sib[rows_of] * theirs
        return [send(ref_sel.at[block_rows(s, j)], x_parts.at[s, j - 1], first_at[s](j)) for j in order]

    def narrow(s, copies):
        for copy in copies:
            copy.wait_recv()
        x_sum[s] = ref_sel[block_rows(s, 0)] + x_parts[s, 0] + x_parts[s, 1] + x_parts[s, 2]
        return [send(x_sum.at[s, bit_rows(s, j)], y_parts.at[s, j - 1], second_at[s](j)) for j in order]

    def settle(s, copies):
        for copy in copies:
            copy.wait_recv()
        carried[own_bit(s)] = x_sum[s, bit_rows(s, 0)] + y_parts[s, 0] + y_parts[s, 1] + y_parts[s, 2]
        return [send(carried.at[own_bit(s)], carried.at[own_bit(s)], second_at[s](j)) for j in order]

    def widen(s, copies):
        for copy in copies:
            copy.wait_recv()
        here = carried.at[block_rows(s, 0)]
        return {j: send(here, here, first_at[s](j)) for j in order}, send(here, here, sibling)

    chosen = [choose(0), choose(1)]
    near.update({(o, 1): send(v_hbm, v_near.at[slot_of(-o)], at_chip(o)) for o in (1, -1)})

    get_q.wait()
    get_k.wait()
    get_v.wait()
    absorb(k_near.at[own], v_near.at[own], None)
    for copy in to_sib:
        copy.wait_recv()
    absorb_near(5 - core)

    far, passed = {}, []
    for part, hold in ((0, k_near), (1, v_near)):
        for o in (1, -1):
            near[o, part].wait_recv()
            got = hold.at[slot_of(-o)]
            far[o, part] = send(got, hold.at[slot_of(-2 * o)], at_chip(o))
            passed.append(send(got, got, sibling))
    absorb_two(slot_of(-1), slot_of(1))

    narrowed = [narrow(s, chosen[s]) for s in (0, 1)]

    for copy in passed:
        copy.wait_recv()
    absorb_two(3 - core, 7 - core)

    settled = [settle(s, narrowed[s]) for s in (0, 1)]

    for copy in far.values():
        copy.wait_recv()
    gone = 8 - 7 * core
    last = [send(hold.at[gone], hold.at[gone], sibling) for hold in (k_near, v_near)]
    absorb_two(core, 8 + core)

    widened = [widen(s, settled[s]) for s in (0, 1)]

    for copy in last:
        copy.wait_recv()
    absorb_near(1 + 7 * core)

    def absorb_style(j):
        def body(s, carry):
            axis = jnp.where(s == 0, x, y)
            there = pl.ds(pl.multiple_of(s * 4 * block + lax.rem(axis + j, 4) * block, block), block)
            absorb(style.at[0, there], style.at[1, there], None)
            return carry

        lax.fori_loop(0, 2, body, 0)

    for s in (0, 1):
        widened[s][1].wait_recv()
    absorb_style(0)
    for j in order:
        shown = []
        for s in (0, 1):
            widened[s][0][j].wait_recv()
            there = carried.at[block_rows(s, 4 - j)]
            shown.append(send(there, there, sibling))
        for copy in shown:
            copy.wait_recv()
        absorb_style(4 - j)

    for h in range(heads):
        att[:, pl.ds(h * HD, HD)] = (acc[h] / total[h]).T.astype(jnp.bfloat16)

    get_w.wait()
    parts = width // LANES
    signs = (1, -1)

    def share(ahead, some):
        cols = pl.ds(pl.multiple_of(lax.rem(z + ahead + 8, 8) * width, LANES), width)
        return dot(att[some, :], w_buf[:, cols], ((1,), (0,)))

    def hop(way, step, part):
        i = (step * 2 + way) * parts + part
        some = pl.ds(way * half, half) if step == 0 else pl.ds(0, rows)
        return pltpu.make_async_remote_copy(
            src_ref=z_out.at[step, way, part, some], dst_ref=z_in.at[step, way, part, some],
            send_sem=z_send.at[i], recv_sem=z_recv.at[i],
            device_id=at_z(signs[way]), device_id_type=MESH,
        )

    whole = pl.ds(0, rows)
    for step in range(4):
        for way in (0, 1):
            some = pl.ds(way * half, half) if step == 0 else whole
            mine_here = share(signs[way] * (4 - step), some)
            for part in range(parts):
                value = mine_here[:, part * LANES : (part + 1) * LANES]
                if step == 0:
                    z_out[step, way, part, some] = value.astype(jnp.bfloat16)
                elif step == 1:
                    hop(way, 0, part).wait_recv()
                    for piece_of in (0, 1):
                        here = pl.ds(piece_of * half, half)
                        one = value[piece_of * half : (piece_of + 1) * half]
                        if piece_of == way:
                            one = one + z_in[0, way, part, here].astype(jnp.float32)
                        z_out[step, way, part, here] = one.astype(jnp.bfloat16)
                else:
                    hop(way, step - 1, part).wait_recv()
                    z_out[step, way, part] = (value + z_in[step - 1, way, part].astype(jnp.float32)).astype(
                        jnp.bfloat16
                    )
                hop(way, step, part).start()

    get_res.wait()
    mine_here = share(0, whole)
    for part in range(parts):
        cols = pl.ds(part * LANES, LANES)
        value = mine_here[:, part * LANES : (part + 1) * LANES]
        for way in (0, 1):
            hop(way, 3, part).wait_recv()
            value = value + z_in[3, way, part].astype(jnp.float32)
        out_ref[:, cols] = (res_buf[:, cols].astype(jnp.float32) + gate_ref[:, cols] * value).astype(jnp.bfloat16)

    for copy in made:
        copy.wait_send()
    for step in range(4):
        for way in (0, 1):
            for part in range(parts):
                hop(way, step, part).wait_send()


def per_device(
    queries, key_rows, value_rows, ref_keys, ref_values, key_lists, list_counts, owner_index, out_weight, residual,
    gate_scale,
):
    rows, width = queries.shape
    heads = width // HD
    ref_rows = ref_keys.shape[1]
    block, bit = ref_rows // 8, ref_rows // 32
    bf16, f32 = jnp.bfloat16, jnp.float32
    hbm = pl.BlockSpec(memory_space=pl.ANY)
    vmem = pl.BlockSpec(memory_space=pltpu.VMEM)
    smem = pl.BlockSpec(memory_space=pltpu.SMEM)
    copies = 64
    hops = 4 * 2 * (width // LANES)
    return pl.pallas_call(
        kernel,
        out_shape=jax.ShapeDtypeStruct((rows, width), bf16),
        in_specs=[hbm] * 5 + [smem] * 3 + [hbm, hbm, vmem],
        out_specs=vmem,
        scratch_shapes=[
            pltpu.VMEM((rows, width), bf16),
            pltpu.VMEM((10, rows, width), bf16),
            pltpu.VMEM((10, rows, width), bf16),
            pltpu.VMEM((ref_rows, width), bf16),
            pltpu.VMEM((ref_rows, width), bf16),
            pltpu.VMEM((ref_rows, width), bf16),
            pltpu.VMEM((2, 3, block, width), bf16),
            pltpu.VMEM((2, block, width), bf16),
            pltpu.VMEM((2, 3, bit, width), bf16),
            pltpu.VMEM((2, ref_rows, width), bf16),
            pltpu.VMEM(out_weight.shape, bf16),
            pltpu.VMEM((rows, width), bf16),
            pltpu.VMEM((heads, 1, rows), f32),
            pltpu.VMEM((heads, 1, rows), f32),
            pltpu.VMEM((heads, HD, rows), f32),
            pltpu.VMEM((rows, width), bf16),
            pltpu.VMEM((4, 2, width // LANES, rows, LANES), bf16),
            pltpu.VMEM((4, 2, width // LANES, rows, LANES), bf16),
            pltpu.SemaphoreType.DMA((7,)),
            pltpu.SemaphoreType.DMA((copies,)),
            pltpu.SemaphoreType.DMA((copies,)),
            pltpu.SemaphoreType.DMA((hops,)),
            pltpu.SemaphoreType.DMA((hops,)),
        ],
        compiler_params=pltpu.CompilerParams(
            collective_id=0, has_side_effects=True, vmem_limit_bytes=60 * 1024 * 1024
        ),
        name="block",
    )(
        queries, key_rows, value_rows, ref_keys, ref_values, key_lists, list_counts, owner_index, out_weight,
        residual, gate_scale.reshape(1, width),
    )


def solution(mesh):
    placed = (
        P("frame", "head"),
        P("frame", "head"),
        P("frame", "head"),
        P("frame", None, "head"),
        P("frame", None, "head"),
        P("frame", None),
        P("frame"),
        P(),
        P("head", None),
        P("frame", "head"),
        P("head"),
    )
    return jax.shard_map(
        per_device, mesh=mesh, in_specs=placed, out_specs=P("frame", "head"), check_vma=False
    )
```

```python
import math

import jax
import jax.numpy as jnp
from jax import lax
from jax.experimental import pallas as pl
from jax.experimental.pallas import tpu as pltpu
from jax.sharding import PartitionSpec as P

HD = 128
REACH = 4
MESH = pl.DeviceIdType.MESH
SCALE = math.log2(math.e) / math.sqrt(HD)
FAR = 1e30
LANES = 128


def dot(a, b, dims):
    return lax.dot_general(a, b, (dims, ((), ())), preferred_element_type=jnp.float32)


def kernel(
    q_hbm, k_hbm, v_hbm, rk_hbm, rv_hbm, lists, counts, owner, w_hbm,
    out_ref,
    q_buf, k_near, v_near, ref_own, ref_sib, ref_sel, x_parts, x_sum, y_parts, style,
    w_sum, w_all, top, total, acc, att, att_all, z_out, z_in, local_sem, send_sem, recv_sem, z_send, z_recv,
):
    rows, width = q_buf.shape
    slots = lists.shape[1]
    ref_rows = style.shape[1]
    half = rows // 2
    block, bit = ref_rows // 8, ref_rows // 32
    early = w_sum.shape[0]
    cols = (pl.ds(0, early), pl.ds(early, width - early))
    heads = (tuple(range(early // HD)), tuple(range(early // HD, width // HD)))
    late = width - early

    frame = lax.axis_index("frame")
    z = lax.axis_index("head")
    core = lax.rem(frame, 2)
    chip = frame // 2
    x, y = chip // 4, lax.rem(chip, 4)
    sibling = (frame + 1 - 2 * core, z)

    def at_x(j):
        return (lax.rem(x + j, 4) * 8 + y * 2 + core, z)

    def at_y(j):
        return (x * 8 + lax.rem(y + j, 4) * 2 + core, z)

    def at_chip(o):
        return (lax.rem(chip + o + 16, 16) * 2 + core, z)

    def ahead(o):
        return lax.rem(z + o + 8, 8)

    def at_z(o):
        return (frame, ahead(o))

    made = []

    def remote(src, dst, device):
        i = len(made)
        copy = pltpu.make_async_remote_copy(
            src_ref=src, dst_ref=dst, send_sem=send_sem.at[i], recv_sem=recv_sem.at[i],
            device_id=device, device_id_type=MESH,
        )
        made.append(copy)
        return copy

    def send(src, dst, device):
        copy = remote(src, dst, device)
        copy.start()
        return copy

    def fetch(src, dst, i):
        copy = pltpu.make_async_copy(src, dst, local_sem.at[i])
        copy.start()
        return copy

    own = 4 + core
    get_q = fetch(q_hbm, q_buf, 0)
    get_k = fetch(k_hbm, k_near.at[own], 1)
    get_v = fetch(v_hbm, v_near.at[own], 2)

    style_in = ((rk_hbm, rv_hbm), (rv_hbm, rk_hbm))

    def half_rows(s):
        return pl.ds(s * 4 * block, 4 * block)

    def keep(s, which):
        return pltpu.make_async_copy(
            style_in[which][0].at[0, half_rows(s)], ref_own.at[half_rows(s)], local_sem.at[3 + s]
        )

    def give(s, w, which, i):
        return pltpu.make_async_remote_copy(
            src_ref=style_in[which][1].at[0, half_rows(s), cols[w]], dst_ref=ref_sib.at[half_rows(s), cols[w]],
            send_sem=send_sem.at[i], recv_sem=recv_sem.at[i], device_id=sibling, device_id_type=MESH,
        )

    for which in (0, 1):

        @pl.when(core == which)
        def _():
            for s in (0, 1):
                keep(s, which).start()

    get_w = fetch(w_hbm.at[pl.ds(0, early)], w_sum, 5)

    def column_block(o):
        return pl.ds(pl.multiple_of(ahead(o) * width, LANES), width)

    get_own_w = fetch(w_hbm.at[pl.ds(early, late), column_block(0)], w_all.at[z], 6)

    barrier = pltpu.get_barrier_semaphore()
    partners = (
        [sibling]
        + [at_x(j) for j in (1, 2, 3)]
        + [at_y(j) for j in (1, 2, 3)]
        + [at_chip(o) for o in (1, -1)]
        + [at_z(o) for o in range(1, 8)]
    )
    for device in partners:
        pl.semaphore_signal(barrier, inc=1, device_id=device, device_id_type=MESH)
    pl.semaphore_wait(barrier, len(partners))

    gifts = [(s, w) for w in (0, 1) for s in (0, 1)]
    for which in (0, 1):

        @pl.when(core == which)
        def _():
            for i, (s, w) in enumerate(gifts):
                give(s, w, which, i).start()

    made += [give(s, w, 0, i) for i, (s, w) in enumerate(gifts)]
    given = {(s, w): made[i] for i, (s, w) in enumerate(gifts)}

    to_sib = [send(k_hbm, k_near.at[own], sibling), send(v_hbm, v_near.at[own], sibling)]

    def slot_of(o):
        return (o + 2) * 2 + core

    near, far, passed, gone = {}, {}, {}, {}

    def to_next(w, hbm, hold):
        for o in (1, -1):
            near[w, o, hbm is k_hbm] = send(hbm.at[:, cols[w]], hold.at[slot_of(-o), :, cols[w]], at_chip(o))

    def relay(w):
        passed[w], far[w] = [], []
        for hold in (k_near, v_near):
            for o in (1, -1):
                near[w, o, hold is k_near].wait_recv()
                got = hold.at[slot_of(-o), :, cols[w]]
                far[w].append(send(got, hold.at[slot_of(-2 * o), :, cols[w]], at_chip(o)))
                passed[w].append(send(got, got, sibling))

    def relay_far(w):
        for copy in far[w]:
            copy.wait_recv()
        slot = 8 - 7 * core
        gone[w] = [
            send(hold.at[slot, :, cols[w]], hold.at[slot, :, cols[w]], sibling) for hold in (k_near, v_near)
        ]

    to_next(0, k_hbm, k_near)
    w_moves = {
        o: send(w_hbm.at[pl.ds(early, late), column_block(o)], w_all.at[z], at_z(o)) for o in (4, 3, 5, 2, 6, 1, 7)
    }

    top[...] = jnp.full(top.shape, -FAR, jnp.float32)
    total[...] = jnp.zeros(total.shape, jnp.float32)
    acc[...] = jnp.zeros(acc.shape, jnp.float32)

    def absorb(w, blocks):
        for h in heads[w]:
            lanes = pl.ds(h * HD, HD)
            query = q_buf[:, lanes]
            scores = [dot(k_ref[:, lanes], query, ((1,), (1,))) for k_ref, _, _ in blocks]
            before = top[h]
            after = before
            for (_, _, penalty), score in zip(blocks, scores):
                best = jnp.max(score, axis=0, keepdims=True)
                after = jnp.maximum(after, best if penalty is None else best - penalty)
            factor = jnp.exp2((before - after) * SCALE)
            shift = after * SCALE
            weighted = acc[h] * factor
            sums = total[h] * factor
            for (_, v_ref, penalty), score in zip(blocks, scores):
                weights = jnp.exp2(score * SCALE - (shift if penalty is None else shift + penalty))
                sums = sums + jnp.sum(weights, axis=0, keepdims=True)
                weighted = weighted + dot(v_ref[:, lanes], weights.astype(jnp.bfloat16), ((0,), (0,)))
            top[h] = after
            total[h] = sums
            acc[h] = weighted

    def near_block(slot):
        there = frame - core - 4 + slot
        hits = jnp.int32(0)
        for j in range(slots):
            hits += jnp.where((lists[0, j] == there) & (j < counts[0]), 1, 0)
        penalty = jnp.where(hits > 0, jnp.float32(0), jnp.float32(FAR))
        return k_near.at[slot], v_near.at[slot], penalty

    def absorb_near(w, *which):
        absorb(w, [near_block(slot) for slot in which])

    first_axis, first_at, second_axis, second_at = (x, y), (at_x, at_y), (y, x), (at_y, at_x)
    order = (1, 3, 2)
    mine = jnp.where(owner[0] == frame, 1.0, 0.0).astype(jnp.bfloat16)
    theirs = jnp.where(owner[0] == frame + 1 - 2 * core, 1.0, 0.0).astype(jnp.bfloat16)
    carried = style.at[core]

    def block_rows(s, j):
        return pl.ds(pl.multiple_of(s * 4 * block + lax.rem(first_axis[s] + j, 4) * block, block), block)

    def bit_rows(s, j):
        return pl.ds(pl.multiple_of(lax.rem(second_axis[s] + j, 4) * bit, bit), bit)

    def own_bit(s):
        return pl.ds(
            pl.multiple_of(s * 4 * block + first_axis[s] * block + second_axis[s] * bit, bit), bit
        )

    chosen, narrowed, settled, widened, shown = {}, {}, {}, {}, {}

    def choose(s, w):
        c, r = cols[w], half_rows(s)
        if w == 0:
            keep(s, 0).wait()
        given[s, w].wait_recv()
        ref_sel[r, c] = ref_own[r, c] * mine + ref_sib[r, c] * theirs
        chosen[s, w] = [
            send(ref_sel.at[block_rows(s, j), c], x_parts.at[s, j - 1, :, c], first_at[s](j)) for j in order
        ]

    def narrow(s, w):
        c = cols[w]
        for copy in chosen[s, w]:
            copy.wait_recv()
        x_sum[s, :, c] = (
            ref_sel[block_rows(s, 0), c] + x_parts[s, 0, :, c] + x_parts[s, 1, :, c] + x_parts[s, 2, :, c]
        )
        narrowed[s, w] = [
            send(x_sum.at[s, bit_rows(s, j), c], y_parts.at[s, j - 1, :, c], second_at[s](j)) for j in order
        ]

    def settle(s, w):
        c = cols[w]
        for copy in narrowed[s, w]:
            copy.wait_recv()
        carried[own_bit(s), c] = (
            x_sum[s, bit_rows(s, 0), c] + y_parts[s, 0, :, c] + y_parts[s, 1, :, c] + y_parts[s, 2, :, c]
        )
        here = carried.at[own_bit(s), c]
        settled[s, w] = [send(here, here, second_at[s](j)) for j in order]

    def widen(s, w):
        for copy in settled[s, w]:
            copy.wait_recv()
        here = carried.at[block_rows(s, 0), cols[w]]
        widened[s, w] = {j: send(here, here, first_at[s](j)) for j in order}
        shown[s, w, 0] = send(here, here, sibling)

    def show(s, w, j):
        widened[s, w][j].wait_recv()
        there = carried.at[block_rows(s, 4 - j), cols[w]]
        shown[s, w, j] = send(there, there, sibling)

    def absorb_style(w, j):
        for s in (0, 1):
            shown[s, w, j].wait_recv()
        absorb(w, [(style.at[0, block_rows(s, 4 - j)], style.at[1, block_rows(s, 4 - j)], None) for s in (0, 1)])

    def both(stage, w):
        for s in (0, 1):
            stage(s, w)

    def finish(w):
        for h in heads[w]:
            att[:, pl.ds(h * HD, HD)] = (acc[h] / total[h]).T.astype(jnp.bfloat16)

    parts = width // LANES
    signs = (1, -1)
    whole = pl.ds(0, rows)

    def share(o, some):
        return dot(att[some, cols[0]], w_sum[:, column_block(o)], ((1,), (0,)))

    def hop(way, step, part):
        i = (step * 2 + way) * parts + part
        some = pl.ds(way * half, half) if step == 0 else whole
        return pltpu.make_async_remote_copy(
            src_ref=z_out.at[step, way, part, some], dst_ref=z_in.at[step, way, part, some],
            send_sem=z_send.at[i], recv_sem=z_recv.at[i],
            device_id=at_z(signs[way]), device_id_type=MESH,
        )

    def climb(step):
        for way in (0, 1):
            some = pl.ds(way * half, half) if step == 0 else whole
            here_share = share(signs[way] * (4 - step), some)
            for part in range(parts):
                value = here_share[:, part * LANES : (part + 1) * LANES]
                if step == 0:
                    z_out[step, way, part, some] = value.astype(jnp.bfloat16)
                elif step == 1:
                    hop(way, 0, part).wait_recv()
                    for which in (0, 1):
                        here = pl.ds(which * half, half)
                        one = value[which * half : (which + 1) * half]
                        if which == way:
                            one = one + z_in[0, way, part, here].astype(jnp.float32)
                        z_out[step, way, part, here] = one.astype(jnp.bfloat16)
                else:
                    hop(way, step - 1, part).wait_recv()
                    z_out[step, way, part] = (value + z_in[step - 1, way, part].astype(jnp.float32)).astype(
                        jnp.bfloat16
                    )
                hop(way, step, part).start()

    spread = {}

    def gather_near():
        mine_here = att.at[:, cols[1]]
        for o in (2, -2, 1, -1):
            spread[o] = send(mine_here, att_all.at[z], at_z(o))

    def gather_far():
        for way in (0, 1):
            o = signs[way]
            spread[2 * o].wait_recv()
            origin = ahead(-2 * o)
            some = pl.ds(way * half, half)
            spread[4 * o] = send(att_all.at[origin, some], att_all.at[origin, some], at_z(2 * o))
            spread[3 * o] = send(att_all.at[origin], att_all.at[origin], at_z(o))

    def late_share(o):
        return dot(att_all[ahead(o)], w_all[ahead(o)], ((1,), (0,)))

    both(choose, 0)
    to_next(0, v_hbm, v_near)
    get_q.wait()
    get_k.wait()
    get_v.wait()
    for copy in to_sib:
        copy.wait_recv()
    absorb(0, [(k_near.at[own], v_near.at[own], None), near_block(5 - core)])
    relay(0)
    to_next(1, k_hbm, k_near)
    to_next(1, v_hbm, v_near)
    both(choose, 1)
    absorb(1, [(k_near.at[own], v_near.at[own], None), near_block(5 - core)])
    both(narrow, 0)
    absorb_near(0, slot_of(-1), slot_of(1))
    both(settle, 0)
    both(narrow, 1)
    for copy in passed[0]:
        copy.wait_recv()
    absorb_near(0, 3 - core, 7 - core)
    both(widen, 0)
    both(settle, 1)
    relay_far(0)
    relay(1)
    absorb_near(0, slot_of(-2), slot_of(2))
    both(widen, 1)
    for copy in gone[0]:
        copy.wait_recv()
    absorb_near(0, 1 + 7 * core)
    absorb_style(0, 0)
    for j in order:
        for s in (0, 1):
            show(s, 0, j)
        absorb_style(0, j)
    finish(0)
    get_w.wait()
    climb(0)
    absorb_near(1, slot_of(-1), slot_of(1))
    for copy in passed[1]:
        copy.wait_recv()
    absorb_near(1, 3 - core, 7 - core)
    climb(1)
    relay_far(1)
    absorb_near(1, slot_of(-2), slot_of(2))
    absorb_style(1, 0)
    for j in order:
        for s in (0, 1):
            show(s, 1, j)
    climb(2)
    for copy in gone[1]:
        copy.wait_recv()
    absorb_near(1, 1 + 7 * core)
    for j in order:
        absorb_style(1, j)
    finish(1)
    gather_near()
    climb(3)
    att_all[z] = att[:, cols[1]]
    get_own_w.wait()
    for copy in w_moves.values():
        copy.wait_recv()
    out_ref[...] = share(0, whole) + late_share(0)
    gather_far()
    for o in (1, -1):
        spread[o].wait_recv()
    out_ref[...] += late_share(1) + late_share(-1) + late_share(2) + late_share(-2)
    for part in range(parts):
        lanes = pl.ds(part * LANES, LANES)
        for way in (0, 1):
            hop(way, 3, part).wait_recv()
        out_ref[:, lanes] += z_in[3, 0, part].astype(jnp.float32) + z_in[3, 1, part].astype(jnp.float32)
    for o in (3, -3, 4, -4):
        spread[o].wait_recv()
    out_ref[...] += late_share(3) + late_share(-3) + late_share(4)

    for copy in made:
        copy.wait_send()
    for step in range(4):
        for way in (0, 1):
            for part in range(parts):
                hop(way, step, part).wait_send()


def per_device(
    queries, key_rows, value_rows, ref_keys, ref_values, key_lists, list_counts, owner_index, out_weight, residual,
    gate_scale,
):
    rows, width = queries.shape
    heads = width // HD
    early = (heads - 1) * HD
    ref_rows = ref_keys.shape[1]
    block, bit = ref_rows // 8, ref_rows // 32
    bf16, f32 = jnp.bfloat16, jnp.float32
    hbm = pl.BlockSpec(memory_space=pl.ANY)
    vmem = pl.BlockSpec(memory_space=pltpu.VMEM)
    smem = pl.BlockSpec(memory_space=pltpu.SMEM)
    copies = 128
    hops = 4 * 2 * (width // LANES)
    projected = pl.pallas_call(
        kernel,
        out_shape=jax.ShapeDtypeStruct((rows, width), f32),
        in_specs=[hbm] * 5 + [smem] * 3 + [hbm],
        out_specs=vmem,
        scratch_shapes=[
            pltpu.VMEM((rows, width), bf16),
            pltpu.VMEM((10, rows, width), bf16),
            pltpu.VMEM((10, rows, width), bf16),
            pltpu.VMEM((ref_rows, width), bf16),
            pltpu.VMEM((ref_rows, width), bf16),
            pltpu.VMEM((ref_rows, width), bf16),
            pltpu.VMEM((2, 3, block, width), bf16),
            pltpu.VMEM((2, block, width), bf16),
            pltpu.VMEM((2, 3, bit, width), bf16),
            pltpu.VMEM((2, ref_rows, width), bf16),
            pltpu.VMEM((early, out_weight.shape[1]), bf16),
            pltpu.VMEM((8, width - early, width), bf16),
            pltpu.VMEM((heads, 1, rows), f32),
            pltpu.VMEM((heads, 1, rows), f32),
            pltpu.VMEM((heads, HD, rows), f32),
            pltpu.VMEM((rows, width), bf16),
            pltpu.VMEM((8, rows, width - early), bf16),
            pltpu.VMEM((4, 2, width // LANES, rows, LANES), bf16),
            pltpu.VMEM((4, 2, width // LANES, rows, LANES), bf16),
            pltpu.SemaphoreType.DMA((7,)),
            pltpu.SemaphoreType.DMA((copies,)),
            pltpu.SemaphoreType.DMA((copies,)),
            pltpu.SemaphoreType.DMA((hops,)),
            pltpu.SemaphoreType.DMA((hops,)),
        ],
        compiler_params=pltpu.CompilerParams(
            collective_id=0, has_side_effects=True, vmem_limit_bytes=60 * 1024 * 1024
        ),
        name="block",
    )(
        queries, key_rows, value_rows, ref_keys, ref_values, key_lists, list_counts, owner_index, out_weight,
    )
    return (residual.astype(f32) + gate_scale[None, :] * projected).astype(bf16)


def solution(mesh):
    placed = (
        P("frame", "head"),
        P("frame", "head"),
        P("frame", "head"),
        P("frame", None, "head"),
        P("frame", None, "head"),
        P("frame", None),
        P("frame"),
        P(),
        P("head", None),
        P("frame", "head"),
        P("head"),
    )
    return jax.shard_map(
        per_device, mesh=mesh, in_specs=placed, out_specs=P("frame", "head"), check_vma=False
    )
```

```python
import math

import jax
import jax.numpy as jnp
from jax import lax
from jax.experimental import pallas as pl
from jax.experimental.pallas import tpu as pltpu
from jax.sharding import PartitionSpec as P

HD = 128
REACH = 4
MESH = pl.DeviceIdType.MESH
SCALE = math.log2(math.e) / math.sqrt(HD)
FAR = 1e30
LANES = 128


def dot(a, b, dims):
    return lax.dot_general(a, b, (dims, ((), ())), preferred_element_type=jnp.float32)


def kernel(
    q_hbm, k_hbm, v_hbm, rk_hbm, rv_hbm, lists, counts, owner, w_hbm,
    out_ref,
    q_buf, k_near, v_near, ref_own, ref_sib, ref_sel, x_parts, x_sum, y_parts, style,
    w_sum, top, total, acc, att, z_out, z_in, local_sem, send_sem, recv_sem, z_send, z_recv,
):
    rows, width = q_buf.shape
    slots = lists.shape[1]
    ref_rows = style.shape[1]
    half = rows // 2
    block, bit = ref_rows // 8, ref_rows // 32
    cols, heads = (pl.ds(0, width),), (tuple(range(width // HD)),)

    frame = lax.axis_index("frame")
    z = lax.axis_index("head")
    core = lax.rem(frame, 2)
    chip = frame // 2
    x, y = chip // 4, lax.rem(chip, 4)
    sibling = (frame + 1 - 2 * core, z)

    def at_x(j):
        return (lax.rem(x + j, 4) * 8 + y * 2 + core, z)

    def at_y(j):
        return (x * 8 + lax.rem(y + j, 4) * 2 + core, z)

    def at_chip(o):
        return (lax.rem(chip + o + 16, 16) * 2 + core, z)

    def ahead(o):
        return lax.rem(z + o + 8, 8)

    def at_z(o):
        return (frame, ahead(o))

    made = []

    def remote(src, dst, device):
        i = len(made)
        copy = pltpu.make_async_remote_copy(
            src_ref=src, dst_ref=dst, send_sem=send_sem.at[i], recv_sem=recv_sem.at[i],
            device_id=device, device_id_type=MESH,
        )
        made.append(copy)
        return copy

    def send(src, dst, device):
        copy = remote(src, dst, device)
        copy.start()
        return copy

    def fetch(src, dst, i):
        copy = pltpu.make_async_copy(src, dst, local_sem.at[i])
        copy.start()
        return copy

    own = 4 + core
    get_q = fetch(q_hbm, q_buf, 0)
    get_k = fetch(k_hbm, k_near.at[own], 1)
    get_v = fetch(v_hbm, v_near.at[own], 2)

    style_in = ((rk_hbm, rv_hbm), (rv_hbm, rk_hbm))

    def half_rows(s):
        return pl.ds(s * 4 * block, 4 * block)

    def keep(s, which):
        return pltpu.make_async_copy(
            style_in[which][0].at[0, half_rows(s)], ref_own.at[half_rows(s)], local_sem.at[3 + s]
        )

    def give(s, w, which, i):
        return pltpu.make_async_remote_copy(
            src_ref=style_in[which][1].at[0, half_rows(s), cols[w]], dst_ref=ref_sib.at[half_rows(s), cols[w]],
            send_sem=send_sem.at[i], recv_sem=recv_sem.at[i], device_id=sibling, device_id_type=MESH,
        )

    for which in (0, 1):

        @pl.when(core == which)
        def _():
            for s in (0, 1):
                keep(s, which).start()

    get_w = fetch(w_hbm, w_sum, 5)

    def column_block(o):
        return pl.ds(pl.multiple_of(ahead(o) * width, LANES), width)

    barrier = pltpu.get_barrier_semaphore()
    partners = (
        [sibling]
        + [at_x(j) for j in (1, 2, 3)]
        + [at_y(j) for j in (1, 2, 3)]
        + [at_chip(o) for o in (1, -1)]
        + [at_z(1), at_z(-1)]
    )
    for device in partners:
        pl.semaphore_signal(barrier, inc=1, device_id=device, device_id_type=MESH)
    pl.semaphore_wait(barrier, len(partners))

    gifts = [(s, w) for w in (0,) for s in (0, 1)]
    for which in (0, 1):

        @pl.when(core == which)
        def _():
            for i, (s, w) in enumerate(gifts):
                give(s, w, which, i).start()

    made += [give(s, w, 0, i) for i, (s, w) in enumerate(gifts)]
    given = {(s, w): made[i] for i, (s, w) in enumerate(gifts)}

    to_sib = [send(k_hbm, k_near.at[own], sibling), send(v_hbm, v_near.at[own], sibling)]

    def slot_of(o):
        return (o + 2) * 2 + core

    near, far, passed, gone = {}, {}, {}, {}

    def to_next(w, hbm, hold):
        for o in (1, -1):
            near[w, o, hbm is k_hbm] = send(hbm.at[:, cols[w]], hold.at[slot_of(-o), :, cols[w]], at_chip(o))

    def relay(w):
        passed[w], far[w] = [], []
        for hold in (k_near, v_near):
            for o in (1, -1):
                near[w, o, hold is k_near].wait_recv()
                got = hold.at[slot_of(-o), :, cols[w]]
                far[w].append(send(got, hold.at[slot_of(-2 * o), :, cols[w]], at_chip(o)))
                passed[w].append(send(got, got, sibling))

    def relay_far(w):
        for copy in far[w]:
            copy.wait_recv()
        slot = 8 - 7 * core
        gone[w] = [
            send(hold.at[slot, :, cols[w]], hold.at[slot, :, cols[w]], sibling) for hold in (k_near, v_near)
        ]

    to_next(0, k_hbm, k_near)

    top[...] = jnp.full(top.shape, -FAR, jnp.float32)
    total[...] = jnp.zeros(total.shape, jnp.float32)
    acc[...] = jnp.zeros(acc.shape, jnp.float32)

    def absorb(w, blocks):
        for h in heads[w]:
            lanes = pl.ds(h * HD, HD)
            query = q_buf[:, lanes]
            scores = [dot(k_ref[:, lanes], query, ((1,), (1,))) for k_ref, _, _ in blocks]
            before = top[h]
            after = before
            for (_, _, penalty), score in zip(blocks, scores):
                best = jnp.max(score, axis=0, keepdims=True)
                after = jnp.maximum(after, best if penalty is None else best - penalty)
            factor = jnp.exp2((before - after) * SCALE)
            shift = after * SCALE
            weighted = acc[h] * factor
            sums = total[h] * factor
            for (_, v_ref, penalty), score in zip(blocks, scores):
                weights = jnp.exp2(score * SCALE - (shift if penalty is None else shift + penalty))
                sums = sums + jnp.sum(weights, axis=0, keepdims=True)
                weighted = weighted + dot(v_ref[:, lanes], weights.astype(jnp.bfloat16), ((0,), (0,)))
            top[h] = after
            total[h] = sums
            acc[h] = weighted

    def near_block(slot):
        there = frame - core - 4 + slot
        hits = jnp.int32(0)
        for j in range(slots):
            hits += jnp.where((lists[0, j] == there) & (j < counts[0]), 1, 0)
        penalty = jnp.where(hits > 0, jnp.float32(0), jnp.float32(FAR))
        return k_near.at[slot], v_near.at[slot], penalty

    def absorb_near(w, *which):
        absorb(w, [near_block(slot) for slot in which])

    first_axis, first_at, second_axis, second_at = (x, y), (at_x, at_y), (y, x), (at_y, at_x)
    order = (1, 3, 2)
    mine = jnp.where(owner[0] == frame, 1.0, 0.0).astype(jnp.bfloat16)
    theirs = jnp.where(owner[0] == frame + 1 - 2 * core, 1.0, 0.0).astype(jnp.bfloat16)
    carried = style.at[core]

    def block_rows(s, j):
        return pl.ds(pl.multiple_of(s * 4 * block + lax.rem(first_axis[s] + j, 4) * block, block), block)

    def bit_rows(s, j):
        return pl.ds(pl.multiple_of(lax.rem(second_axis[s] + j, 4) * bit, bit), bit)

    def own_bit(s):
        return pl.ds(
            pl.multiple_of(s * 4 * block + first_axis[s] * block + second_axis[s] * bit, bit), bit
        )

    chosen, narrowed, settled, widened, shown = {}, {}, {}, {}, {}

    def choose(s, w):
        c, r = cols[w], half_rows(s)
        if w == 0:
            keep(s, 0).wait()
        given[s, w].wait_recv()
        ref_sel[r, c] = ref_own[r, c] * mine + ref_sib[r, c] * theirs
        chosen[s, w] = [
            send(ref_sel.at[block_rows(s, j), c], x_parts.at[s, j - 1, :, c], first_at[s](j)) for j in order
        ]

    def narrow(s, w):
        c = cols[w]
        for copy in chosen[s, w]:
            copy.wait_recv()
        x_sum[s, :, c] = (
            ref_sel[block_rows(s, 0), c] + x_parts[s, 0, :, c] + x_parts[s, 1, :, c] + x_parts[s, 2, :, c]
        )
        narrowed[s, w] = [
            send(x_sum.at[s, bit_rows(s, j), c], y_parts.at[s, j - 1, :, c], second_at[s](j)) for j in order
        ]

    def settle(s, w):
        c = cols[w]
        for copy in narrowed[s, w]:
            copy.wait_recv()
        carried[own_bit(s), c] = (
            x_sum[s, bit_rows(s, 0), c] + y_parts[s, 0, :, c] + y_parts[s, 1, :, c] + y_parts[s, 2, :, c]
        )
        here = carried.at[own_bit(s), c]
        settled[s, w] = [send(here, here, second_at[s](j)) for j in order]

    def widen(s, w):
        for copy in settled[s, w]:
            copy.wait_recv()
        here = carried.at[block_rows(s, 0), cols[w]]
        widened[s, w] = {j: send(here, here, first_at[s](j)) for j in order}
        shown[s, w, 0] = send(here, here, sibling)

    def show(s, w, j):
        widened[s, w][j].wait_recv()
        there = carried.at[block_rows(s, 4 - j), cols[w]]
        shown[s, w, j] = send(there, there, sibling)

    def absorb_style(w, j):
        for s in (0, 1):
            shown[s, w, j].wait_recv()
        absorb(w, [(style.at[0, block_rows(s, 4 - j)], style.at[1, block_rows(s, 4 - j)], None) for s in (0, 1)])

    def both(stage, w):
        for s in (0, 1):
            stage(s, w)

    def finish(w):
        for h in heads[w]:
            att[:, pl.ds(h * HD, HD)] = (acc[h] / total[h]).T.astype(jnp.bfloat16)

    parts = width // LANES
    signs = (1, -1)
    whole = pl.ds(0, rows)

    def share(o, some):
        return dot(att[some, cols[0]], w_sum[:, column_block(o)], ((1,), (0,)))

    def hop(way, step, part):
        i = (step * 2 + way) * parts + part
        some = pl.ds(way * half, half) if step == 0 else whole
        return pltpu.make_async_remote_copy(
            src_ref=z_out.at[step, way, part, some], dst_ref=z_in.at[step, way, part, some],
            send_sem=z_send.at[i], recv_sem=z_recv.at[i],
            device_id=at_z(signs[way]), device_id_type=MESH,
        )

    def climb(step):
        for way in (0, 1):
            some = pl.ds(way * half, half) if step == 0 else whole
            here_share = share(signs[way] * (4 - step), some)
            for part in range(parts):
                value = here_share[:, part * LANES : (part + 1) * LANES]
                if step == 0:
                    z_out[step, way, part, some] = value.astype(jnp.bfloat16)
                elif step == 1:
                    hop(way, 0, part).wait_recv()
                    for which in (0, 1):
                        here = pl.ds(which * half, half)
                        one = value[which * half : (which + 1) * half]
                        if which == way:
                            one = one + z_in[0, way, part, here].astype(jnp.float32)
                        z_out[step, way, part, here] = one.astype(jnp.bfloat16)
                else:
                    hop(way, step - 1, part).wait_recv()
                    z_out[step, way, part] = (value + z_in[step - 1, way, part].astype(jnp.float32)).astype(
                        jnp.bfloat16
                    )
                hop(way, step, part).start()

    both(choose, 0)
    get_q.wait()
    get_k.wait()
    get_v.wait()
    for copy in to_sib:
        copy.wait_recv()
    absorb(0, [(k_near.at[own], v_near.at[own], None), near_block(5 - core)])
    to_next(0, v_hbm, v_near)
    both(narrow, 0)
    relay(0)
    absorb_near(0, slot_of(-1), slot_of(1))
    both(settle, 0)
    for copy in passed[0]:
        copy.wait_recv()
    absorb_near(0, 3 - core, 7 - core)
    both(widen, 0)
    relay_far(0)
    absorb_near(0, slot_of(-2), slot_of(2))
    for copy in gone[0]:
        copy.wait_recv()
    absorb_near(0, 1 + 7 * core)
    absorb_style(0, 0)
    for j in order:
        for s in (0, 1):
            show(s, 0, j)
        absorb_style(0, j)
    finish(0)
    get_w.wait()
    for step in range(4):
        climb(step)
    out_ref[...] = share(0, whole)
    for part in range(parts):
        lanes = pl.ds(part * LANES, LANES)
        for way in (0, 1):
            hop(way, 3, part).wait_recv()
        out_ref[:, lanes] += z_in[3, 0, part].astype(jnp.float32) + z_in[3, 1, part].astype(jnp.float32)

    for copy in made:
        copy.wait_send()
    for step in range(4):
        for way in (0, 1):
            for part in range(parts):
                hop(way, step, part).wait_send()


def per_device(
    queries, key_rows, value_rows, ref_keys, ref_values, key_lists, list_counts, owner_index, out_weight, residual,
    gate_scale,
):
    rows, width = queries.shape
    heads = width // HD
    ref_rows = ref_keys.shape[1]
    block, bit = ref_rows // 8, ref_rows // 32
    bf16, f32 = jnp.bfloat16, jnp.float32
    hbm = pl.BlockSpec(memory_space=pl.ANY)
    vmem = pl.BlockSpec(memory_space=pltpu.VMEM)
    smem = pl.BlockSpec(memory_space=pltpu.SMEM)
    copies = 72
    hops = 4 * 2 * (width // LANES)
    projected = pl.pallas_call(
        kernel,
        out_shape=jax.ShapeDtypeStruct((rows, width), f32),
        in_specs=[hbm] * 5 + [smem] * 3 + [hbm],
        out_specs=vmem,
        scratch_shapes=[
            pltpu.VMEM((rows, width), bf16),
            pltpu.VMEM((10, rows, width), bf16),
            pltpu.VMEM((10, rows, width), bf16),
            pltpu.VMEM((ref_rows, width), bf16),
            pltpu.VMEM((ref_rows, width), bf16),
            pltpu.VMEM((ref_rows, width), bf16),
            pltpu.VMEM((2, 3, block, width), bf16),
            pltpu.VMEM((2, block, width), bf16),
            pltpu.VMEM((2, 3, bit, width), bf16),
            pltpu.VMEM((2, ref_rows, width), bf16),
            pltpu.VMEM(out_weight.shape, bf16),
            pltpu.VMEM((heads, 1, rows), f32),
            pltpu.VMEM((heads, 1, rows), f32),
            pltpu.VMEM((heads, HD, rows), f32),
            pltpu.VMEM((rows, width), bf16),
            pltpu.VMEM((4, 2, width // LANES, rows, LANES), bf16),
            pltpu.VMEM((4, 2, width // LANES, rows, LANES), bf16),
            pltpu.SemaphoreType.DMA((7,)),
            pltpu.SemaphoreType.DMA((copies,)),
            pltpu.SemaphoreType.DMA((copies,)),
            pltpu.SemaphoreType.DMA((hops,)),
            pltpu.SemaphoreType.DMA((hops,)),
        ],
        compiler_params=pltpu.CompilerParams(
            collective_id=0, has_side_effects=True, vmem_limit_bytes=60 * 1024 * 1024
        ),
        name="block",
    )(
        queries, key_rows, value_rows, ref_keys, ref_values, key_lists, list_counts, owner_index, out_weight,
    )
    return (residual.astype(f32) + gate_scale[None, :] * projected).astype(bf16)


def solution(mesh):
    placed = (
        P("frame", "head"),
        P("frame", "head"),
        P("frame", "head"),
        P("frame", None, "head"),
        P("frame", None, "head"),
        P("frame", None),
        P("frame"),
        P(),
        P("head", None),
        P("frame", "head"),
        P("head"),
    )
    return jax.shard_map(
        per_device, mesh=mesh, in_specs=placed, out_specs=P("frame", "head"), check_vma=False
    )
```

```python
import math

import jax
import jax.numpy as jnp
from jax import lax
from jax.experimental import pallas as pl
from jax.experimental.pallas import tpu as pltpu
from jax.sharding import PartitionSpec as P

HD = 128
REACH = 4
MESH = pl.DeviceIdType.MESH
SCALE = math.log2(math.e) / math.sqrt(HD)
FAR = 1e30
LANES = 128


def dot(a, b, dims):
    return lax.dot_general(a, b, (dims, ((), ())), preferred_element_type=jnp.float32)


def kernel(
    q_hbm, k_hbm, v_hbm, rk_hbm, rv_hbm, lists, counts, owner, w_hbm,
    out_ref,
    q_buf, k_near, v_near, ref_own, ref_sib, ref_sel, x_parts, x_sum, y_parts, style,
    w_sum, top, total, acc, att, z_out, z_in, local_sem, send_sem, recv_sem, z_send, z_recv,
):
    rows, width = q_buf.shape
    slots = lists.shape[1]
    ref_rows = style.shape[1]
    half = rows // 2
    block, bit = ref_rows // 8, ref_rows // 32
    cols, heads = (pl.ds(0, width),), (tuple(range(width // HD)),)

    frame = lax.axis_index("frame")
    z = lax.axis_index("head")
    core = lax.rem(frame, 2)
    chip = frame // 2
    x, y = chip // 4, lax.rem(chip, 4)
    sibling = (frame + 1 - 2 * core, z)

    def at_x(j):
        return (lax.rem(x + j, 4) * 8 + y * 2 + core, z)

    def at_y(j):
        return (x * 8 + lax.rem(y + j, 4) * 2 + core, z)

    def at_chip(o):
        return (lax.rem(chip + o + 16, 16) * 2 + core, z)

    def ahead(o):
        return lax.rem(z + o + 8, 8)

    def at_z(o):
        return (frame, ahead(o))

    made = []

    def remote(src, dst, device):
        i = len(made)
        copy = pltpu.make_async_remote_copy(
            src_ref=src, dst_ref=dst, send_sem=send_sem.at[i], recv_sem=recv_sem.at[i],
            device_id=device, device_id_type=MESH,
        )
        made.append(copy)
        return copy

    def send(src, dst, device):
        copy = remote(src, dst, device)
        copy.start()
        return copy

    def fetch(src, dst, i):
        copy = pltpu.make_async_copy(src, dst, local_sem.at[i])
        copy.start()
        return copy

    own = 4 + core
    get_q = fetch(q_hbm, q_buf, 0)
    get_k = fetch(k_hbm, k_near.at[own], 1)
    get_v = fetch(v_hbm, v_near.at[own], 2)

    style_in = ((rk_hbm, rv_hbm), (rv_hbm, rk_hbm))

    def half_rows(s):
        return pl.ds(s * 4 * block, 4 * block)

    def keep(s, which):
        return pltpu.make_async_copy(
            style_in[which][0].at[0, half_rows(s)], ref_own.at[half_rows(s)], local_sem.at[3 + s]
        )

    def give(s, w, which, i):
        return pltpu.make_async_remote_copy(
            src_ref=style_in[which][1].at[0, half_rows(s), cols[w]], dst_ref=ref_sib.at[half_rows(s), cols[w]],
            send_sem=send_sem.at[i], recv_sem=recv_sem.at[i], device_id=sibling, device_id_type=MESH,
        )

    for which in (0, 1):

        @pl.when(core == which)
        def _():
            for s in (0, 1):
                keep(s, which).start()

    get_w = fetch(w_hbm, w_sum, 5)

    def column_block(o):
        return pl.ds(pl.multiple_of(ahead(o) * width, LANES), width)

    barrier = pltpu.get_barrier_semaphore()
    partners = (
        [sibling]
        + [at_x(j) for j in (1, 2, 3)]
        + [at_y(j) for j in (1, 2, 3)]
        + [at_chip(o) for o in (1, -1)]
        + [at_z(1), at_z(-1)]
    )
    for device in partners:
        pl.semaphore_signal(barrier, inc=1, device_id=device, device_id_type=MESH)
    pl.semaphore_wait(barrier, len(partners))

    gifts = [(s, w) for w in (0,) for s in (0, 1)]
    for which in (0, 1):

        @pl.when(core == which)
        def _():
            for i, (s, w) in enumerate(gifts):
                give(s, w, which, i).start()

    made += [give(s, w, 0, i) for i, (s, w) in enumerate(gifts)]
    given = {(s, w): made[i] for i, (s, w) in enumerate(gifts)}

    to_sib = [send(k_hbm, k_near.at[own], sibling), send(v_hbm, v_near.at[own], sibling)]

    def slot_of(o):
        return (o + 2) * 2 + core

    near, far, passed, gone = {}, {}, {}, {}

    def to_next(w, hbm, hold):
        for o in (1, -1):
            near[w, o, hbm is k_hbm] = send(hbm.at[:, cols[w]], hold.at[slot_of(-o), :, cols[w]], at_chip(o))

    def relay(w):
        passed[w], far[w] = [], []
        for hold in (k_near, v_near):
            for o in (1, -1):
                near[w, o, hold is k_near].wait_recv()
                got = hold.at[slot_of(-o), :, cols[w]]
                far[w].append(send(got, hold.at[slot_of(-2 * o), :, cols[w]], at_chip(o)))
                passed[w].append(send(got, got, sibling))

    def relay_far(w):
        for copy in far[w]:
            copy.wait_recv()
        slot = 8 - 7 * core
        gone[w] = [
            send(hold.at[slot, :, cols[w]], hold.at[slot, :, cols[w]], sibling) for hold in (k_near, v_near)
        ]

    to_next(0, k_hbm, k_near)

    top[...] = jnp.full(top.shape, -FAR, jnp.float32)
    total[...] = jnp.zeros(total.shape, jnp.float32)
    acc[...] = jnp.zeros(acc.shape, jnp.float32)

    def absorb(w, blocks):
        for h in heads[w]:
            lanes = pl.ds(h * HD, HD)
            query = q_buf[:, lanes]
            scores = [dot(k_ref[:, lanes], query, ((1,), (1,))) for k_ref, _, _ in blocks]
            before = top[h]
            after = before
            for (_, _, penalty), score in zip(blocks, scores):
                best = jnp.max(score, axis=0, keepdims=True)
                after = jnp.maximum(after, best if penalty is None else best - penalty)
            factor = jnp.exp2((before - after) * SCALE)
            shift = after * SCALE
            weighted = acc[h] * factor
            sums = total[h] * factor
            for (_, v_ref, penalty), score in zip(blocks, scores):
                weights = jnp.exp2(score * SCALE - (shift if penalty is None else shift + penalty))
                sums = sums + jnp.sum(weights, axis=0, keepdims=True)
                weighted = weighted + dot(v_ref[:, lanes], weights.astype(jnp.bfloat16), ((0,), (0,)))
            top[h] = after
            total[h] = sums
            acc[h] = weighted

    def near_block(slot):
        there = frame - core - 4 + slot
        hits = jnp.int32(0)
        for j in range(slots):
            hits += jnp.where((lists[0, j] == there) & (j < counts[0]), 1, 0)
        penalty = jnp.where(hits > 0, jnp.float32(0), jnp.float32(FAR))
        return k_near.at[slot], v_near.at[slot], penalty

    def absorb_near(w, *which):
        absorb(w, [near_block(slot) for slot in which])

    first_axis, first_at, second_axis, second_at = (x, y), (at_x, at_y), (y, x), (at_y, at_x)
    order = (1, 3, 2)
    mine = jnp.where(owner[0] == frame, 1.0, 0.0).astype(jnp.bfloat16)
    theirs = jnp.where(owner[0] == frame + 1 - 2 * core, 1.0, 0.0).astype(jnp.bfloat16)
    carried = style.at[core]

    def block_rows(s, j):
        return pl.ds(pl.multiple_of(s * 4 * block + lax.rem(first_axis[s] + j, 4) * block, block), block)

    def bit_rows(s, j):
        return pl.ds(pl.multiple_of(lax.rem(second_axis[s] + j, 4) * bit, bit), bit)

    def own_bit(s):
        return pl.ds(
            pl.multiple_of(s * 4 * block + first_axis[s] * block + second_axis[s] * bit, bit), bit
        )

    chosen, narrowed, settled, widened, shown = {}, {}, {}, {}, {}

    def choose(s, w):
        c, r = cols[w], half_rows(s)
        if w == 0:
            keep(s, 0).wait()
        given[s, w].wait_recv()
        ref_sel[r, c] = ref_own[r, c] * mine + ref_sib[r, c] * theirs
        chosen[s, w] = [
            send(ref_sel.at[block_rows(s, j), c], x_parts.at[s, j - 1, :, c], first_at[s](j)) for j in order
        ]

    def narrow(s, w):
        c = cols[w]
        for copy in chosen[s, w]:
            copy.wait_recv()
        x_sum[s, :, c] = (
            ref_sel[block_rows(s, 0), c] + x_parts[s, 0, :, c] + x_parts[s, 1, :, c] + x_parts[s, 2, :, c]
        )
        narrowed[s, w] = [
            send(x_sum.at[s, bit_rows(s, j), c], y_parts.at[s, j - 1, :, c], second_at[s](j)) for j in order
        ]

    def settle(s, w):
        c = cols[w]
        for copy in narrowed[s, w]:
            copy.wait_recv()
        carried[own_bit(s), c] = (
            x_sum[s, bit_rows(s, 0), c] + y_parts[s, 0, :, c] + y_parts[s, 1, :, c] + y_parts[s, 2, :, c]
        )
        here = carried.at[own_bit(s), c]
        settled[s, w] = [send(here, here, second_at[s](j)) for j in order]

    def widen(s, w):
        for copy in settled[s, w]:
            copy.wait_recv()
        here = carried.at[block_rows(s, 0), cols[w]]
        widened[s, w] = {j: send(here, here, first_at[s](j)) for j in order}
        shown[s, w, 0] = send(here, here, sibling)

    def show(s, w, j):
        widened[s, w][j].wait_recv()
        there = carried.at[block_rows(s, 4 - j), cols[w]]
        shown[s, w, j] = send(there, there, sibling)

    def absorb_style(w, j):
        for s in (0, 1):
            shown[s, w, j].wait_recv()
        absorb(w, [(style.at[0, block_rows(s, 4 - j)], style.at[1, block_rows(s, 4 - j)], None) for s in (0, 1)])

    def both(stage, w):
        for s in (0, 1):
            stage(s, w)

    def finish(w):
        for h in heads[w]:
            att[:, pl.ds(h * HD, HD)] = (acc[h] / total[h]).T.astype(jnp.bfloat16)

    parts = width // LANES
    signs = (1, -1)
    whole = pl.ds(0, rows)

    def share(o, some):
        return dot(att[some, cols[0]], w_sum[:, column_block(o)], ((1,), (0,)))

    def hop(way, step, part):
        i = (step * 2 + way) * parts + part
        some = pl.ds(way * half, half) if step == 0 else whole
        return pltpu.make_async_remote_copy(
            src_ref=z_out.at[step, way, part, some], dst_ref=z_in.at[step, way, part, some],
            send_sem=z_send.at[i], recv_sem=z_recv.at[i],
            device_id=at_z(signs[way]), device_id_type=MESH,
        )

    def climb(step):
        some = [pl.ds(way * half, half) if step == 0 else whole for way in (0, 1)]
        shares = [share(signs[way] * (4 - step), some[way]) for way in (0, 1)]
        for part in range(parts):
            for way in (0, 1):
                value = shares[way][:, part * LANES : (part + 1) * LANES]
                if step == 0:
                    z_out[step, way, part, some[way]] = value.astype(jnp.bfloat16)
                elif step == 1:
                    hop(way, 0, part).wait_recv()
                    for which in (0, 1):
                        here = pl.ds(which * half, half)
                        one = value[which * half : (which + 1) * half]
                        if which == way:
                            one = one + z_in[0, way, part, here].astype(jnp.float32)
                        z_out[step, way, part, here] = one.astype(jnp.bfloat16)
                else:
                    hop(way, step - 1, part).wait_recv()
                    z_out[step, way, part] = (value + z_in[step - 1, way, part].astype(jnp.float32)).astype(
                        jnp.bfloat16
                    )
                hop(way, step, part).start()

    both(choose, 0)
    get_q.wait()
    get_k.wait()
    get_v.wait()
    for copy in to_sib:
        copy.wait_recv()
    absorb(0, [(k_near.at[own], v_near.at[own], None), near_block(5 - core)])
    to_next(0, v_hbm, v_near)
    both(narrow, 0)
    relay(0)
    absorb_near(0, slot_of(-1), slot_of(1))
    both(settle, 0)
    for copy in passed[0]:
        copy.wait_recv()
    absorb_near(0, 3 - core, 7 - core)
    both(widen, 0)
    relay_far(0)
    absorb_near(0, slot_of(-2), slot_of(2))
    for copy in gone[0]:
        copy.wait_recv()
    absorb_near(0, 1 + 7 * core)
    absorb_style(0, 0)
    for s in (0, 1):
        show(s, 0, 1)
    for s in (0, 1):
        show(s, 0, 3)
    absorb_style(0, 1)
    for s in (0, 1):
        show(s, 0, 2)
    absorb_style(0, 3)
    absorb_style(0, 2)
    finish(0)
    get_w.wait()
    for step in range(4):
        climb(step)
    out_ref[...] = share(0, whole)
    for part in range(parts):
        lanes = pl.ds(part * LANES, LANES)
        for way in (0, 1):
            hop(way, 3, part).wait_recv()
        out_ref[:, lanes] += z_in[3, 0, part].astype(jnp.float32) + z_in[3, 1, part].astype(jnp.float32)

    for copy in made:
        copy.wait_send()
    for step in range(4):
        for way in (0, 1):
            for part in range(parts):
                hop(way, step, part).wait_send()


def per_device(
    queries, key_rows, value_rows, ref_keys, ref_values, key_lists, list_counts, owner_index, out_weight, residual,
    gate_scale,
):
    rows, width = queries.shape
    heads = width // HD
    ref_rows = ref_keys.shape[1]
    block, bit = ref_rows // 8, ref_rows // 32
    bf16, f32 = jnp.bfloat16, jnp.float32
    hbm = pl.BlockSpec(memory_space=pl.ANY)
    vmem = pl.BlockSpec(memory_space=pltpu.VMEM)
    smem = pl.BlockSpec(memory_space=pltpu.SMEM)
    copies = 72
    hops = 4 * 2 * (width // LANES)
    projected = pl.pallas_call(
        kernel,
        out_shape=jax.ShapeDtypeStruct((rows, width), f32),
        in_specs=[hbm] * 5 + [smem] * 3 + [hbm],
        out_specs=vmem,
        scratch_shapes=[
            pltpu.VMEM((rows, width), bf16),
            pltpu.VMEM((10, rows, width), bf16),
            pltpu.VMEM((10, rows, width), bf16),
            pltpu.VMEM((ref_rows, width), bf16),
            pltpu.VMEM((ref_rows, width), bf16),
            pltpu.VMEM((ref_rows, width), bf16),
            pltpu.VMEM((2, 3, block, width), bf16),
            pltpu.VMEM((2, block, width), bf16),
            pltpu.VMEM((2, 3, bit, width), bf16),
            pltpu.VMEM((2, ref_rows, width), bf16),
            pltpu.VMEM(out_weight.shape, bf16),
            pltpu.VMEM((heads, 1, rows), f32),
            pltpu.VMEM((heads, 1, rows), f32),
            pltpu.VMEM((heads, HD, rows), f32),
            pltpu.VMEM((rows, width), bf16),
            pltpu.VMEM((4, 2, width // LANES, rows, LANES), bf16),
            pltpu.VMEM((4, 2, width // LANES, rows, LANES), bf16),
            pltpu.SemaphoreType.DMA((7,)),
            pltpu.SemaphoreType.DMA((copies,)),
            pltpu.SemaphoreType.DMA((copies,)),
            pltpu.SemaphoreType.DMA((hops,)),
            pltpu.SemaphoreType.DMA((hops,)),
        ],
        compiler_params=pltpu.CompilerParams(
            collective_id=0, has_side_effects=True, vmem_limit_bytes=60 * 1024 * 1024
        ),
        name="block",
    )(
        queries, key_rows, value_rows, ref_keys, ref_values, key_lists, list_counts, owner_index, out_weight,
    )
    return (residual.astype(f32) + gate_scale[None, :] * projected).astype(bf16)


def solution(mesh):
    placed = (
        P("frame", "head"),
        P("frame", "head"),
        P("frame", "head"),
        P("frame", None, "head"),
        P("frame", None, "head"),
        P("frame", None),
        P("frame"),
        P(),
        P("head", None),
        P("frame", "head"),
        P("head"),
    )
    return jax.shard_map(
        per_device, mesh=mesh, in_specs=placed, out_specs=P("frame", "head"), check_vma=False
    )
```

```python
import math

import jax
import jax.numpy as jnp
from jax import lax
from jax.experimental import pallas as pl
from jax.experimental.pallas import tpu as pltpu
from jax.sharding import PartitionSpec as P

HD = 128
REACH = 4
MESH = pl.DeviceIdType.MESH
SCALE = math.log2(math.e) / math.sqrt(HD)
FAR = 1e30
LANES = 128


def dot(a, b, dims):
    return lax.dot_general(a, b, (dims, ((), ())), preferred_element_type=jnp.float32)


def kernel(
    q_hbm, k_hbm, v_hbm, rk_hbm, rv_hbm, lists, counts, owner, w_hbm,
    out_ref,
    q_buf, k_near, v_near, ref_own, ref_sib, ref_sel, x_parts, x_sum, y_parts, style,
    w_sum, top, total, acc, att, z_out, z_in, local_sem, send_sem, recv_sem, z_send, z_recv,
):
    rows, width = q_buf.shape
    slots = lists.shape[1]
    ref_rows = style.shape[1]
    half = rows // 2
    chains = 4
    base, size = tuple(ref_rows // chains * s for s in range(chains)), (ref_rows // chains,) * chains
    block, bit = tuple(n // 4 for n in size), tuple(n // 16 for n in size)
    cols, heads = (pl.ds(0, width),), (tuple(range(width // HD)),)

    frame = lax.axis_index("frame")
    z = lax.axis_index("head")
    core = lax.rem(frame, 2)
    chip = frame // 2
    x, y = chip // 4, lax.rem(chip, 4)
    sibling = (frame + 1 - 2 * core, z)

    def at_x(j):
        return (lax.rem(x + j, 4) * 8 + y * 2 + core, z)

    def at_y(j):
        return (x * 8 + lax.rem(y + j, 4) * 2 + core, z)

    def at_chip(o):
        return (lax.rem(chip + o + 16, 16) * 2 + core, z)

    def ahead(o):
        return lax.rem(z + o + 8, 8)

    def at_z(o):
        return (frame, ahead(o))

    made = []

    def remote(src, dst, device):
        i = len(made)
        copy = pltpu.make_async_remote_copy(
            src_ref=src, dst_ref=dst, send_sem=send_sem.at[i], recv_sem=recv_sem.at[i],
            device_id=device, device_id_type=MESH,
        )
        made.append(copy)
        return copy

    def send(src, dst, device):
        copy = remote(src, dst, device)
        copy.start()
        return copy

    def fetch(src, dst, i):
        copy = pltpu.make_async_copy(src, dst, local_sem.at[i])
        copy.start()
        return copy

    own = 4 + core
    sooner, later = (0, 2), (1, 3)
    get_q = fetch(q_hbm, q_buf, 0)
    get_k = fetch(k_hbm, k_near.at[own], 1)
    get_v = fetch(v_hbm, v_near.at[own], 2)

    style_in = ((rk_hbm, rv_hbm), (rv_hbm, rk_hbm))

    def half_rows(s):
        return pl.ds(base[s], size[s])

    def keep(s, which):
        return pltpu.make_async_copy(
            style_in[which][0].at[0, half_rows(s)], ref_own.at[half_rows(s)], local_sem.at[3 + s]
        )

    def give(s, w, which, i):
        return pltpu.make_async_remote_copy(
            src_ref=style_in[which][1].at[0, half_rows(s), cols[w]], dst_ref=ref_sib.at[half_rows(s), cols[w]],
            send_sem=send_sem.at[i], recv_sem=recv_sem.at[i], device_id=sibling, device_id_type=MESH,
        )

    for which in (0, 1):

        @pl.when(core == which)
        def _():
            for s in sooner + later:
                keep(s, which).start()

    get_w = fetch(w_hbm, w_sum, 7)

    def column_block(o):
        return pl.ds(pl.multiple_of(ahead(o) * width, LANES), width)

    barrier = pltpu.get_barrier_semaphore()
    partners = (
        [sibling]
        + [at_x(j) for j in (1, 2, 3)]
        + [at_y(j) for j in (1, 2, 3)]
        + [at_chip(o) for o in (1, -1)]
        + [at_z(1), at_z(-1)]
    )
    for device in partners:
        pl.semaphore_signal(barrier, inc=1, device_id=device, device_id_type=MESH)
    pl.semaphore_wait(barrier, len(partners))

    gifts = [(s, w) for w in (0,) for s in sooner + later]
    for which in (0, 1):

        @pl.when(core == which)
        def _():
            for i, (s, w) in enumerate(gifts):
                give(s, w, which, i).start()

    made += [give(s, w, 0, i) for i, (s, w) in enumerate(gifts)]
    given = {(s, w): made[i] for i, (s, w) in enumerate(gifts)}

    to_sib = [send(k_hbm, k_near.at[own], sibling), send(v_hbm, v_near.at[own], sibling)]

    def slot_of(o):
        return (o + 2) * 2 + core

    near, far, passed, gone = {}, {}, {}, {}

    def to_next(w, hbm, hold):
        for o in (1, -1):
            near[w, o, hbm is k_hbm] = send(hbm.at[:, cols[w]], hold.at[slot_of(-o), :, cols[w]], at_chip(o))

    def relay(w):
        passed[w], far[w] = [], []
        for hold in (k_near, v_near):
            for o in (1, -1):
                near[w, o, hold is k_near].wait_recv()
                got = hold.at[slot_of(-o), :, cols[w]]
                far[w].append(send(got, hold.at[slot_of(-2 * o), :, cols[w]], at_chip(o)))
                passed[w].append(send(got, got, sibling))

    def relay_far(w):
        for copy in far[w]:
            copy.wait_recv()
        slot = 8 - 7 * core
        gone[w] = [
            send(hold.at[slot, :, cols[w]], hold.at[slot, :, cols[w]], sibling) for hold in (k_near, v_near)
        ]

    to_next(0, k_hbm, k_near)

    top[...] = jnp.full(top.shape, -FAR, jnp.float32)
    total[...] = jnp.zeros(total.shape, jnp.float32)
    acc[...] = jnp.zeros(acc.shape, jnp.float32)

    def absorb(w, blocks):
        for h in heads[w]:
            lanes = pl.ds(h * HD, HD)
            query = q_buf[:, lanes]
            scores = [dot(k_ref[:, lanes], query, ((1,), (1,))) for k_ref, _, _ in blocks]
            before = top[h]
            after = before
            for (_, _, penalty), score in zip(blocks, scores):
                best = jnp.max(score, axis=0, keepdims=True)
                after = jnp.maximum(after, best if penalty is None else best - penalty)
            factor = jnp.exp2((before - after) * SCALE)
            shift = after * SCALE
            weighted = acc[h] * factor
            sums = total[h] * factor
            for (_, v_ref, penalty), score in zip(blocks, scores):
                weights = jnp.exp2(score * SCALE - (shift if penalty is None else shift + penalty))
                sums = sums + jnp.sum(weights, axis=0, keepdims=True)
                weighted = weighted + dot(v_ref[:, lanes], weights.astype(jnp.bfloat16), ((0,), (0,)))
            top[h] = after
            total[h] = sums
            acc[h] = weighted

    def near_block(slot):
        there = frame - core - 4 + slot
        hits = jnp.int32(0)
        for j in range(slots):
            hits += jnp.where((lists[0, j] == there) & (j < counts[0]), 1, 0)
        penalty = jnp.where(hits > 0, jnp.float32(0), jnp.float32(FAR))
        return k_near.at[slot], v_near.at[slot], penalty

    def absorb_near(w, *which):
        absorb(w, [near_block(slot) for slot in which])

    first_axis, first_at = (x, x, y, y), (at_x, at_x, at_y, at_y)
    second_axis, second_at = (y, y, x, x), (at_y, at_y, at_x, at_x)
    order = (1, 3, 2)
    mine = jnp.where(owner[0] == frame, 1.0, 0.0).astype(jnp.bfloat16)
    theirs = jnp.where(owner[0] == frame + 1 - 2 * core, 1.0, 0.0).astype(jnp.bfloat16)
    carried = style.at[core]

    def block_rows(s, j):
        return pl.ds(pl.multiple_of(base[s] + lax.rem(first_axis[s] + j, 4) * block[s], bit[s]), block[s])

    def bit_rows(s, j):
        return pl.ds(pl.multiple_of(lax.rem(second_axis[s] + j, 4) * bit[s], bit[s]), bit[s])

    def own_bit(s):
        return pl.ds(
            pl.multiple_of(base[s] + first_axis[s] * block[s] + second_axis[s] * bit[s], bit[s]), bit[s]
        )

    whole_block = tuple(pl.ds(0, n) for n in block)
    whole_bit = tuple(pl.ds(0, n) for n in bit)
    chosen, narrowed, settled, widened, shown = {}, {}, {}, {}, {}

    def choose(s, w):
        c, r = cols[w], half_rows(s)
        if w == 0:
            keep(s, 0).wait()
        given[s, w].wait_recv()
        ref_sel[r, c] = ref_own[r, c] * mine + ref_sib[r, c] * theirs
        chosen[s, w] = [
            send(ref_sel.at[block_rows(s, j), c], x_parts.at[s, j - 1, whole_block[s], c], first_at[s](j)) for j in order
        ]

    def narrow(s, w):
        c = cols[w]
        for copy in chosen[s, w]:
            copy.wait_recv()
        b = whole_block[s]
        x_sum[s, b, c] = (
            ref_sel[block_rows(s, 0), c] + x_parts[s, 0, b, c] + x_parts[s, 1, b, c] + x_parts[s, 2, b, c]
        )
        narrowed[s, w] = [
            send(x_sum.at[s, bit_rows(s, j), c], y_parts.at[s, j - 1, whole_bit[s], c], second_at[s](j)) for j in order
        ]

    def settle(s, w):
        c = cols[w]
        for copy in narrowed[s, w]:
            copy.wait_recv()
        b = whole_bit[s]
        carried[own_bit(s), c] = (
            x_sum[s, bit_rows(s, 0), c] + y_parts[s, 0, b, c] + y_parts[s, 1, b, c] + y_parts[s, 2, b, c]
        )
        here = carried.at[own_bit(s), c]
        settled[s, w] = [send(here, here, second_at[s](j)) for j in order]

    def widen(s, w):
        for copy in settled[s, w]:
            copy.wait_recv()
        here = carried.at[block_rows(s, 0), cols[w]]
        widened[s, w] = {j: send(here, here, first_at[s](j)) for j in order}
        shown[s, w, 0] = send(here, here, sibling)

    def show(s, w, j):
        widened[s, w][j].wait_recv()
        there = carried.at[block_rows(s, 4 - j), cols[w]]
        shown[s, w, j] = send(there, there, sibling)

    def absorb_style(w, j):
        for s in range(chains):
            shown[s, w, j].wait_recv()
        absorb(
            w, [(style.at[0, block_rows(s, 4 - j)], style.at[1, block_rows(s, 4 - j)], None) for s in range(chains)]
        )

    def both(stage, which):
        for s in which:
            stage(s, 0)

    def finish(w):
        for h in heads[w]:
            att[:, pl.ds(h * HD, HD)] = (acc[h] / total[h]).T.astype(jnp.bfloat16)

    parts = width // LANES
    signs = (1, -1)
    whole = pl.ds(0, rows)

    def share(o, some):
        return dot(att[some, cols[0]], w_sum[:, column_block(o)], ((1,), (0,)))

    def hop(way, step, part):
        i = (step * 2 + way) * parts + part
        some = pl.ds(way * half, half) if step == 0 else whole
        return pltpu.make_async_remote_copy(
            src_ref=z_out.at[step, way, part, some], dst_ref=z_in.at[step, way, part, some],
            send_sem=z_send.at[i], recv_sem=z_recv.at[i],
            device_id=at_z(signs[way]), device_id_type=MESH,
        )

    def climb(step):
        some = [pl.ds(way * half, half) if step == 0 else whole for way in (0, 1)]
        shares = [share(signs[way] * (4 - step), some[way]) for way in (0, 1)]
        for part in range(parts):
            for way in (0, 1):
                value = shares[way][:, part * LANES : (part + 1) * LANES]
                if step == 0:
                    z_out[step, way, part, some[way]] = value.astype(jnp.bfloat16)
                elif step == 1:
                    hop(way, 0, part).wait_recv()
                    for which in (0, 1):
                        here = pl.ds(which * half, half)
                        one = value[which * half : (which + 1) * half]
                        if which == way:
                            one = one + z_in[0, way, part, here].astype(jnp.float32)
                        z_out[step, way, part, here] = one.astype(jnp.bfloat16)
                else:
                    hop(way, step - 1, part).wait_recv()
                    z_out[step, way, part] = (value + z_in[step - 1, way, part].astype(jnp.float32)).astype(
                        jnp.bfloat16
                    )
                hop(way, step, part).start()

    both(choose, sooner)
    both(choose, later)
    get_q.wait()
    get_k.wait()
    get_v.wait()
    for copy in to_sib:
        copy.wait_recv()
    absorb(0, [(k_near.at[own], v_near.at[own], None), near_block(5 - core)])
    to_next(0, v_hbm, v_near)
    both(narrow, sooner)
    both(narrow, later)
    relay(0)
    absorb_near(0, slot_of(-1), slot_of(1))
    both(settle, sooner)
    both(settle, later)
    for copy in passed[0]:
        copy.wait_recv()
    absorb_near(0, 3 - core, 7 - core)
    both(widen, sooner)
    both(widen, later)
    relay_far(0)
    absorb_near(0, slot_of(-2), slot_of(2))
    for copy in gone[0]:
        copy.wait_recv()
    absorb_near(0, 1 + 7 * core)
    absorb_style(0, 0)
    for j in (1, 3):
        for s in sooner + later:
            show(s, 0, j)
    absorb_style(0, 1)
    for s in sooner + later:
        show(s, 0, 2)
    absorb_style(0, 3)
    absorb_style(0, 2)
    finish(0)
    get_w.wait()
    for step in range(4):
        climb(step)
    out_ref[...] = share(0, whole)
    for part in range(parts):
        lanes = pl.ds(part * LANES, LANES)
        for way in (0, 1):
            hop(way, 3, part).wait_recv()
        out_ref[:, lanes] += z_in[3, 0, part].astype(jnp.float32) + z_in[3, 1, part].astype(jnp.float32)

    for copy in made:
        copy.wait_send()
    for step in range(4):
        for way in (0, 1):
            for part in range(parts):
                hop(way, step, part).wait_send()


def per_device(
    queries, key_rows, value_rows, ref_keys, ref_values, key_lists, list_counts, owner_index, out_weight, residual,
    gate_scale,
):
    rows, width = queries.shape
    heads = width // HD
    ref_rows = ref_keys.shape[1]
    block, bit = ref_rows // 16, ref_rows // 64
    bf16, f32 = jnp.bfloat16, jnp.float32
    hbm = pl.BlockSpec(memory_space=pl.ANY)
    vmem = pl.BlockSpec(memory_space=pltpu.VMEM)
    smem = pl.BlockSpec(memory_space=pltpu.SMEM)
    copies = 96
    hops = 4 * 2 * (width // LANES)
    projected = pl.pallas_call(
        kernel,
        out_shape=jax.ShapeDtypeStruct((rows, width), f32),
        in_specs=[hbm] * 5 + [smem] * 3 + [hbm],
        out_specs=vmem,
        scratch_shapes=[
            pltpu.VMEM((rows, width), bf16),
            pltpu.VMEM((10, rows, width), bf16),
            pltpu.VMEM((10, rows, width), bf16),
            pltpu.VMEM((ref_rows, width), bf16),
            pltpu.VMEM((ref_rows, width), bf16),
            pltpu.VMEM((ref_rows, width), bf16),
            pltpu.VMEM((4, 3, block, width), bf16),
            pltpu.VMEM((4, block, width), bf16),
            pltpu.VMEM((4, 3, bit, width), bf16),
            pltpu.VMEM((2, ref_rows, width), bf16),
            pltpu.VMEM(out_weight.shape, bf16),
            pltpu.VMEM((heads, 1, rows), f32),
            pltpu.VMEM((heads, 1, rows), f32),
            pltpu.VMEM((heads, HD, rows), f32),
            pltpu.VMEM((rows, width), bf16),
            pltpu.VMEM((4, 2, width // LANES, rows, LANES), bf16),
            pltpu.VMEM((4, 2, width // LANES, rows, LANES), bf16),
            pltpu.SemaphoreType.DMA((8,)),
            pltpu.SemaphoreType.DMA((copies,)),
            pltpu.SemaphoreType.DMA((copies,)),
            pltpu.SemaphoreType.DMA((hops,)),
            pltpu.SemaphoreType.DMA((hops,)),
        ],
        compiler_params=pltpu.CompilerParams(
            collective_id=0, has_side_effects=True, vmem_limit_bytes=60 * 1024 * 1024
        ),
        name="block",
    )(
        queries, key_rows, value_rows, ref_keys, ref_values, key_lists, list_counts, owner_index, out_weight,
    )
    return (residual.astype(f32) + gate_scale[None, :] * projected).astype(bf16)


def solution(mesh):
    placed = (
        P("frame", "head"),
        P("frame", "head"),
        P("frame", "head"),
        P("frame", None, "head"),
        P("frame", None, "head"),
        P("frame", None),
        P("frame"),
        P(),
        P("head", None),
        P("frame", "head"),
        P("head"),
    )
    return jax.shard_map(
        per_device, mesh=mesh, in_specs=placed, out_specs=P("frame", "head"), check_vma=False
    )
```

```python
import math

import jax
import jax.numpy as jnp
from jax import lax
from jax.experimental import pallas as pl
from jax.experimental.pallas import tpu as pltpu
from jax.sharding import PartitionSpec as P

HD = 128
REACH = 4
MESH = pl.DeviceIdType.MESH
SCALE = math.log2(math.e) / math.sqrt(HD)
FAR = 1e30
LANES = 128


def dot(a, b, dims):
    return lax.dot_general(a, b, (dims, ((), ())), preferred_element_type=jnp.float32)


def kernel(
    q_hbm, k_hbm, v_hbm, rk_hbm, rv_hbm, lists, counts, owner, w_hbm,
    out_ref,
    q_buf, k_near, v_near, ref_own, ref_sib, ref_sel, x_parts, x_sum, y_parts, style,
    w_sum, top, total, acc, att, z_out, z_in, local_sem, send_sem, recv_sem, z_send, z_recv,
):
    rows, width = q_buf.shape
    slots = lists.shape[1]
    ref_rows = style.shape[1]
    half = rows // 2
    chains = 4
    base, size = tuple(ref_rows // chains * s for s in range(chains)), (ref_rows // chains,) * chains
    block, bit = tuple(n // 4 for n in size), tuple(n // 16 for n in size)
    cols, heads = (pl.ds(0, width),), (tuple(range(width // HD)),)

    frame = lax.axis_index("frame")
    z = lax.axis_index("head")
    core = lax.rem(frame, 2)
    chip = frame // 2
    x, y = chip // 4, lax.rem(chip, 4)
    sibling = (frame + 1 - 2 * core, z)

    def at_x(j):
        return (lax.rem(x + j, 4) * 8 + y * 2 + core, z)

    def at_y(j):
        return (x * 8 + lax.rem(y + j, 4) * 2 + core, z)

    def at_chip(o):
        return (lax.rem(chip + o + 16, 16) * 2 + core, z)

    def ahead(o):
        return lax.rem(z + o + 8, 8)

    def at_z(o):
        return (frame, ahead(o))

    made = []

    def remote(src, dst, device):
        i = len(made)
        copy = pltpu.make_async_remote_copy(
            src_ref=src, dst_ref=dst, send_sem=send_sem.at[i], recv_sem=recv_sem.at[i],
            device_id=device, device_id_type=MESH,
        )
        made.append(copy)
        return copy

    def send(src, dst, device):
        copy = remote(src, dst, device)
        copy.start()
        return copy

    def fetch(src, dst, i):
        copy = pltpu.make_async_copy(src, dst, local_sem.at[i])
        copy.start()
        return copy

    own = 4 + core
    sooner, later = (0, 2), (1, 3)
    get_q = fetch(q_hbm, q_buf, 0)
    get_k = fetch(k_hbm, k_near.at[own], 1)
    get_v = fetch(v_hbm, v_near.at[own], 2)

    style_in = ((rk_hbm, rv_hbm), (rv_hbm, rk_hbm))

    def half_rows(s):
        return pl.ds(base[s], size[s])

    def keep(s, which):
        return pltpu.make_async_copy(
            style_in[which][0].at[0, half_rows(s)], ref_own.at[half_rows(s)], local_sem.at[3 + s]
        )

    def give(s, w, which, i):
        return pltpu.make_async_remote_copy(
            src_ref=style_in[which][1].at[0, half_rows(s), cols[w]], dst_ref=ref_sib.at[half_rows(s), cols[w]],
            send_sem=send_sem.at[i], recv_sem=recv_sem.at[i], device_id=sibling, device_id_type=MESH,
        )

    for which in (0, 1):

        @pl.when(core == which)
        def _():
            for s in sooner + later:
                keep(s, which).start()

    get_w = fetch(w_hbm, w_sum, 7)

    def column_block(o):
        return pl.ds(pl.multiple_of(ahead(o) * width, LANES), width)

    barrier = pltpu.get_barrier_semaphore()
    partners = (
        [sibling]
        + [at_x(j) for j in (1, 2, 3)]
        + [at_y(j) for j in (1, 2, 3)]
        + [at_chip(o) for o in (1, -1)]
        + [at_z(1), at_z(-1)]
    )
    for device in partners:
        pl.semaphore_signal(barrier, inc=1, device_id=device, device_id_type=MESH)
    pl.semaphore_wait(barrier, len(partners))

    gifts = [(s, w) for w in (0,) for s in sooner + later]
    for which in (0, 1):

        @pl.when(core == which)
        def _():
            for i, (s, w) in enumerate(gifts):
                give(s, w, which, i).start()

    made += [give(s, w, 0, i) for i, (s, w) in enumerate(gifts)]
    given = {(s, w): made[i] for i, (s, w) in enumerate(gifts)}

    to_sib = [send(k_hbm, k_near.at[own], sibling), send(v_hbm, v_near.at[own], sibling)]

    def slot_of(o):
        return (o + 2) * 2 + core

    near, far, passed, gone = {}, {}, {}, {}

    def to_next(w, hbm, hold):
        for o in (1, -1):
            near[w, o, hbm is k_hbm] = send(hbm.at[:, cols[w]], hold.at[slot_of(-o), :, cols[w]], at_chip(o))

    def relay(w):
        passed[w], far[w] = [], []
        for hold in (k_near, v_near):
            for o in (1, -1):
                near[w, o, hold is k_near].wait_recv()
                got = hold.at[slot_of(-o), :, cols[w]]
                far[w].append(send(got, hold.at[slot_of(-2 * o), :, cols[w]], at_chip(o)))
                passed[w].append(send(got, got, sibling))

    def relay_far(w):
        for copy in far[w]:
            copy.wait_recv()
        slot = 8 - 7 * core
        gone[w] = [
            send(hold.at[slot, :, cols[w]], hold.at[slot, :, cols[w]], sibling) for hold in (k_near, v_near)
        ]

    to_next(0, k_hbm, k_near)

    top[...] = jnp.full(top.shape, -FAR, jnp.float32)
    total[...] = jnp.zeros(total.shape, jnp.float32)
    acc[...] = jnp.zeros(acc.shape, jnp.float32)

    def absorb(w, blocks):
        for h in heads[w]:
            lanes = pl.ds(h * HD, HD)
            query = q_buf[:, lanes]
            scores = [dot(k_ref[:, lanes], query, ((1,), (1,))) for k_ref, _, _ in blocks]
            before = top[h]
            after = before
            for (_, _, penalty), score in zip(blocks, scores):
                best = jnp.max(score, axis=0, keepdims=True)
                after = jnp.maximum(after, best if penalty is None else best - penalty)
            factor = jnp.exp2((before - after) * SCALE)
            shift = after * SCALE
            weighted = acc[h] * factor
            sums = total[h] * factor
            for (_, v_ref, penalty), score in zip(blocks, scores):
                weights = jnp.exp2(score * SCALE - (shift if penalty is None else shift + penalty))
                sums = sums + jnp.sum(weights, axis=0, keepdims=True)
                weighted = weighted + dot(v_ref[:, lanes], weights.astype(jnp.bfloat16), ((0,), (0,)))
            top[h] = after
            total[h] = sums
            acc[h] = weighted

    def near_block(slot):
        there = frame - core - 4 + slot
        hits = jnp.int32(0)
        for j in range(slots):
            hits += jnp.where((lists[0, j] == there) & (j < counts[0]), 1, 0)
        penalty = jnp.where(hits > 0, jnp.float32(0), jnp.float32(FAR))
        return k_near.at[slot], v_near.at[slot], penalty

    def absorb_near(w, *which):
        absorb(w, [near_block(slot) for slot in which])

    first_axis, first_at = (x, x, y, y), (at_x, at_x, at_y, at_y)
    second_axis, second_at = (y, y, x, x), (at_y, at_y, at_x, at_x)
    order = (1, 3, 2)
    mine = jnp.where(owner[0] == frame, 1.0, 0.0).astype(jnp.bfloat16)
    theirs = jnp.where(owner[0] == frame + 1 - 2 * core, 1.0, 0.0).astype(jnp.bfloat16)
    carried = style.at[core]

    def block_rows(s, j):
        return pl.ds(pl.multiple_of(base[s] + lax.rem(first_axis[s] + j, 4) * block[s], bit[s]), block[s])

    def bit_rows(s, j):
        return pl.ds(pl.multiple_of(lax.rem(second_axis[s] + j, 4) * bit[s], bit[s]), bit[s])

    def place_of(s, j):
        first = s - s % 2
        return base[first] + lax.rem(first_axis[s] + j, 4) * (2 * block[s]) + s % 2 * block[s]

    def place(s, j):
        return pl.ds(pl.multiple_of(place_of(s, j), block[s]), block[s])

    def own_bit(s):
        return pl.ds(pl.multiple_of(place_of(s, 0) + second_axis[s] * bit[s], bit[s]), bit[s])

    whole_block = tuple(pl.ds(0, n) for n in block)
    whole_bit = tuple(pl.ds(0, n) for n in bit)
    chosen, narrowed, settled, widened, shown = {}, {}, {}, {}, {}

    def choose(s, w):
        c, r = cols[w], half_rows(s)
        if w == 0:
            keep(s, 0).wait()
        given[s, w].wait_recv()
        ref_sel[r, c] = ref_own[r, c] * mine + ref_sib[r, c] * theirs
        chosen[s, w] = [
            send(ref_sel.at[block_rows(s, j), c], x_parts.at[s, j - 1, whole_block[s], c], first_at[s](j)) for j in order
        ]

    def narrow(s, w):
        c = cols[w]
        for copy in chosen[s, w]:
            copy.wait_recv()
        b = whole_block[s]
        x_sum[s, b, c] = (
            ref_sel[block_rows(s, 0), c] + x_parts[s, 0, b, c] + x_parts[s, 1, b, c] + x_parts[s, 2, b, c]
        )
        narrowed[s, w] = [
            send(x_sum.at[s, bit_rows(s, j), c], y_parts.at[s, j - 1, whole_bit[s], c], second_at[s](j)) for j in order
        ]

    def settle(s, w):
        c = cols[w]
        for copy in narrowed[s, w]:
            copy.wait_recv()
        b = whole_bit[s]
        carried[own_bit(s), c] = (
            x_sum[s, bit_rows(s, 0), c] + y_parts[s, 0, b, c] + y_parts[s, 1, b, c] + y_parts[s, 2, b, c]
        )
        here = carried.at[own_bit(s), c]
        settled[s, w] = [send(here, here, second_at[s](j)) for j in order]

    def widen(s, w):
        for copy in settled[s, w]:
            copy.wait_recv()
        here = carried.at[place(s, 0), cols[w]]
        widened[s, w] = {j: send(here, here, first_at[s](j)) for j in order}
        shown[s, w, 0] = send(here, here, sibling)

    def show(s, w, j):
        widened[s, w][j].wait_recv()
        there = carried.at[place(s, 4 - j), cols[w]]
        shown[s, w, j] = send(there, there, sibling)

    def absorb_style(w, j):
        for s in range(chains):
            shown[s, w, j].wait_recv()
        blocks = []
        for s in range(0, chains, 2):
            rows_of = pl.ds(pl.multiple_of(place_of(s, 4 - j), 2 * block[s]), 2 * block[s])
            blocks.append((style.at[0, rows_of], style.at[1, rows_of], None))
        absorb(w, blocks)

    def both(stage, which):
        for s in which:
            stage(s, 0)

    def finish(w):
        for h in heads[w]:
            att[:, pl.ds(h * HD, HD)] = (acc[h] / total[h]).T.astype(jnp.bfloat16)

    parts = width // LANES
    signs = (1, -1)
    whole = pl.ds(0, rows)

    def share(o, some):
        return dot(att[some, cols[0]], w_sum[:, column_block(o)], ((1,), (0,)))

    def hop(way, step, part):
        i = (step * 2 + way) * parts + part
        some = pl.ds(way * half, half) if step == 0 else whole
        return pltpu.make_async_remote_copy(
            src_ref=z_out.at[step, way, part, some], dst_ref=z_in.at[step, way, part, some],
            send_sem=z_send.at[i], recv_sem=z_recv.at[i],
            device_id=at_z(signs[way]), device_id_type=MESH,
        )

    def climb(step):
        some = [pl.ds(way * half, half) if step == 0 else whole for way in (0, 1)]
        shares = [share(signs[way] * (4 - step), some[way]) for way in (0, 1)]
        for part in range(parts):
            for way in (0, 1):
                value = shares[way][:, part * LANES : (part + 1) * LANES]
                if step == 0:
                    z_out[step, way, part, some[way]] = value.astype(jnp.bfloat16)
                elif step == 1:
                    hop(way, 0, part).wait_recv()
                    for which in (0, 1):
                        here = pl.ds(which * half, half)
                        one = value[which * half : (which + 1) * half]
                        if which == way:
                            one = one + z_in[0, way, part, here].astype(jnp.float32)
                        z_out[step, way, part, here] = one.astype(jnp.bfloat16)
                else:
                    hop(way, step - 1, part).wait_recv()
                    z_out[step, way, part] = (value + z_in[step - 1, way, part].astype(jnp.float32)).astype(
                        jnp.bfloat16
                    )
                hop(way, step, part).start()

    both(choose, sooner)
    both(choose, later)
    get_q.wait()
    get_k.wait()
    get_v.wait()
    for copy in to_sib:
        copy.wait_recv()
    absorb(0, [(k_near.at[own], v_near.at[own], None), near_block(5 - core)])
    to_next(0, v_hbm, v_near)
    both(narrow, sooner)
    both(narrow, later)
    relay(0)
    absorb_near(0, slot_of(-1), slot_of(1))
    both(settle, sooner)
    both(settle, later)
    for copy in passed[0]:
        copy.wait_recv()
    absorb_near(0, 3 - core, 7 - core)
    both(widen, sooner)
    both(widen, later)
    relay_far(0)
    absorb_near(0, slot_of(-2), slot_of(2))
    for copy in gone[0]:
        copy.wait_recv()
    absorb_near(0, 1 + 7 * core)
    absorb_style(0, 0)
    for j in (1, 3):
        for s in sooner + later:
            show(s, 0, j)
    absorb_style(0, 1)
    for s in sooner + later:
        show(s, 0, 2)
    absorb_style(0, 3)
    absorb_style(0, 2)
    finish(0)
    get_w.wait()
    for step in range(4):
        climb(step)
    out_ref[...] = share(0, whole)
    for part in range(parts):
        lanes = pl.ds(part * LANES, LANES)
        for way in (0, 1):
            hop(way, 3, part).wait_recv()
        out_ref[:, lanes] += z_in[3, 0, part].astype(jnp.float32) + z_in[3, 1, part].astype(jnp.float32)

    for copy in made:
        copy.wait_send()
    for step in range(4):
        for way in (0, 1):
            for part in range(parts):
                hop(way, step, part).wait_send()


def per_device(
    queries, key_rows, value_rows, ref_keys, ref_values, key_lists, list_counts, owner_index, out_weight, residual,
    gate_scale,
):
    rows, width = queries.shape
    heads = width // HD
    ref_rows = ref_keys.shape[1]
    block, bit = ref_rows // 16, ref_rows // 64
    bf16, f32 = jnp.bfloat16, jnp.float32
    hbm = pl.BlockSpec(memory_space=pl.ANY)
    vmem = pl.BlockSpec(memory_space=pltpu.VMEM)
    smem = pl.BlockSpec(memory_space=pltpu.SMEM)
    copies = 96
    hops = 4 * 2 * (width // LANES)
    projected = pl.pallas_call(
        kernel,
        out_shape=jax.ShapeDtypeStruct((rows, width), f32),
        in_specs=[hbm] * 5 + [smem] * 3 + [hbm],
        out_specs=vmem,
        scratch_shapes=[
            pltpu.VMEM((rows, width), bf16),
            pltpu.VMEM((10, rows, width), bf16),
            pltpu.VMEM((10, rows, width), bf16),
            pltpu.VMEM((ref_rows, width), bf16),
            pltpu.VMEM((ref_rows, width), bf16),
            pltpu.VMEM((ref_rows, width), bf16),
            pltpu.VMEM((4, 3, block, width), bf16),
            pltpu.VMEM((4, block, width), bf16),
            pltpu.VMEM((4, 3, bit, width), bf16),
            pltpu.VMEM((2, ref_rows, width), bf16),
            pltpu.VMEM(out_weight.shape, bf16),
            pltpu.VMEM((heads, 1, rows), f32),
            pltpu.VMEM((heads, 1, rows), f32),
            pltpu.VMEM((heads, HD, rows), f32),
            pltpu.VMEM((rows, width), bf16),
            pltpu.VMEM((4, 2, width // LANES, rows, LANES), bf16),
            pltpu.VMEM((4, 2, width // LANES, rows, LANES), bf16),
            pltpu.SemaphoreType.DMA((8,)),
            pltpu.SemaphoreType.DMA((copies,)),
            pltpu.SemaphoreType.DMA((copies,)),
            pltpu.SemaphoreType.DMA((hops,)),
            pltpu.SemaphoreType.DMA((hops,)),
        ],
        compiler_params=pltpu.CompilerParams(
            collective_id=0, has_side_effects=True, vmem_limit_bytes=60 * 1024 * 1024
        ),
        name="block",
    )(
        queries, key_rows, value_rows, ref_keys, ref_values, key_lists, list_counts, owner_index, out_weight,
    )
    return (residual.astype(f32) + gate_scale[None, :] * projected).astype(bf16)


def solution(mesh):
    placed = (
        P("frame", "head"),
        P("frame", "head"),
        P("frame", "head"),
        P("frame", None, "head"),
        P("frame", None, "head"),
        P("frame", None),
        P("frame"),
        P(),
        P("head", None),
        P("frame", "head"),
        P("head"),
    )
    return jax.shard_map(
        per_device, mesh=mesh, in_specs=placed, out_specs=P("frame", "head"), check_vma=False
    )
```

```python
import math

import jax
import jax.numpy as jnp
from jax import lax
from jax.experimental import pallas as pl
from jax.experimental.pallas import tpu as pltpu
from jax.sharding import PartitionSpec as P

HD = 128
REACH = 4
MESH = pl.DeviceIdType.MESH
SCALE = math.log2(math.e) / math.sqrt(HD)
FAR = 1e30
LANES = 128


def dot(a, b, dims):
    return lax.dot_general(a, b, (dims, ((), ())), preferred_element_type=jnp.float32)


def kernel(
    q_hbm, k_hbm, v_hbm, rk_hbm, rv_hbm, lists, counts, owner, w_hbm,
    out_ref,
    q_buf, k_near, v_near, ref_own, ref_sib, ref_sel, x_parts, x_sum, y_parts, style,
    w_sum, top, total, acc, att, z_out, z_in, local_sem, send_sem, recv_sem, z_send, z_recv,
):
    rows, width = q_buf.shape
    slots = lists.shape[1]
    ref_rows = style.shape[1]
    half = rows // 2
    chains = 4
    base, size = tuple(ref_rows // chains * s for s in range(chains)), (ref_rows // chains,) * chains
    block, bit = tuple(n // 4 for n in size), tuple(n // 16 for n in size)
    cols, heads = (pl.ds(0, width),), (tuple(range(width // HD)),)

    frame = lax.axis_index("frame")
    z = lax.axis_index("head")
    core = lax.rem(frame, 2)
    chip = frame // 2
    x, y = chip // 4, lax.rem(chip, 4)
    sibling = (frame + 1 - 2 * core, z)

    def at_x(j):
        return (lax.rem(x + j, 4) * 8 + y * 2 + core, z)

    def at_y(j):
        return (x * 8 + lax.rem(y + j, 4) * 2 + core, z)

    def at_chip(o):
        return (lax.rem(chip + o + 16, 16) * 2 + core, z)

    def ahead(o):
        return lax.rem(z + o + 8, 8)

    def at_z(o):
        return (frame, ahead(o))

    made = []

    def remote(src, dst, device):
        i = len(made)
        copy = pltpu.make_async_remote_copy(
            src_ref=src, dst_ref=dst, send_sem=send_sem.at[i], recv_sem=recv_sem.at[i],
            device_id=device, device_id_type=MESH,
        )
        made.append(copy)
        return copy

    def send(src, dst, device):
        copy = remote(src, dst, device)
        copy.start()
        return copy

    def fetch(src, dst, i):
        copy = pltpu.make_async_copy(src, dst, local_sem.at[i])
        copy.start()
        return copy

    own = 4 + core
    sooner, later = (0, 2), (1, 3)
    get_q = fetch(q_hbm, q_buf, 0)
    get_k = fetch(k_hbm, k_near.at[own], 1)
    get_v = fetch(v_hbm, v_near.at[own], 2)

    style_in = ((rk_hbm, rv_hbm), (rv_hbm, rk_hbm))

    def half_rows(s):
        return pl.ds(base[s], size[s])

    def keep(s, which):
        return pltpu.make_async_copy(
            style_in[which][0].at[0, half_rows(s)], ref_own.at[half_rows(s)], local_sem.at[3 + s]
        )

    def give(s, w, which, i):
        return pltpu.make_async_remote_copy(
            src_ref=style_in[which][1].at[0, half_rows(s), cols[w]], dst_ref=ref_sib.at[half_rows(s), cols[w]],
            send_sem=send_sem.at[i], recv_sem=recv_sem.at[i], device_id=sibling, device_id_type=MESH,
        )

    for which in (0, 1):

        @pl.when(core == which)
        def _():
            for s in sooner + later:
                keep(s, which).start()

    get_w = fetch(w_hbm, w_sum, 7)

    def column_block(o):
        return pl.ds(pl.multiple_of(ahead(o) * width, LANES), width)

    barrier = pltpu.get_barrier_semaphore()
    partners = (
        [sibling]
        + [at_x(j) for j in (1, 2, 3)]
        + [at_y(j) for j in (1, 2, 3)]
        + [at_chip(o) for o in (1, -1)]
        + [at_z(1), at_z(-1)]
    )
    for device in partners:
        pl.semaphore_signal(barrier, inc=1, device_id=device, device_id_type=MESH)
    pl.semaphore_wait(barrier, len(partners))

    gifts = [(s, w) for w in (0,) for s in sooner + later]
    for which in (0, 1):

        @pl.when(core == which)
        def _():
            for i, (s, w) in enumerate(gifts):
                give(s, w, which, i).start()

    made += [give(s, w, 0, i) for i, (s, w) in enumerate(gifts)]
    given = {(s, w): made[i] for i, (s, w) in enumerate(gifts)}

    to_sib = [send(k_hbm, k_near.at[own], sibling), send(v_hbm, v_near.at[own], sibling)]

    def slot_of(o):
        return (o + 2) * 2 + core

    near, far, passed, gone = {}, {}, {}, {}

    def to_next(w, hbm, hold):
        for o in (1, -1):
            near[w, o, hbm is k_hbm] = send(hbm.at[:, cols[w]], hold.at[slot_of(-o), :, cols[w]], at_chip(o))

    def relay(w):
        passed[w], far[w] = [], []
        for hold in (k_near, v_near):
            for o in (1, -1):
                near[w, o, hold is k_near].wait_recv()
                got = hold.at[slot_of(-o), :, cols[w]]
                far[w].append(send(got, hold.at[slot_of(-2 * o), :, cols[w]], at_chip(o)))
                passed[w].append(send(got, got, sibling))

    def relay_far(w):
        for copy in far[w]:
            copy.wait_recv()
        slot = 8 - 7 * core
        gone[w] = [
            send(hold.at[slot, :, cols[w]], hold.at[slot, :, cols[w]], sibling) for hold in (k_near, v_near)
        ]

    to_next(0, k_hbm, k_near)

    top[...] = jnp.full(top.shape, -FAR, jnp.float32)
    total[...] = jnp.zeros(total.shape, jnp.float32)
    acc[...] = jnp.zeros(acc.shape, jnp.float32)

    def absorb(w, blocks):
        for h in heads[w]:
            lanes = pl.ds(h * HD, HD)
            query = q_buf[:, lanes]
            scores = [dot(k_ref[:, lanes], query, ((1,), (1,))) for k_ref, _, _ in blocks]
            before = top[h]
            after = before
            for (_, _, penalty), score in zip(blocks, scores):
                best = jnp.max(score, axis=0, keepdims=True)
                after = jnp.maximum(after, best if penalty is None else best - penalty)
            factor = jnp.exp2((before - after) * SCALE)
            shift = after * SCALE
            weighted = acc[h] * factor
            sums = total[h] * factor
            for (_, v_ref, penalty), score in zip(blocks, scores):
                weights = jnp.exp2(score * SCALE - (shift if penalty is None else shift + penalty))
                sums = sums + jnp.sum(weights, axis=0, keepdims=True)
                weighted = weighted + dot(v_ref[:, lanes], weights.astype(jnp.bfloat16), ((0,), (0,)))
            top[h] = after
            total[h] = sums
            acc[h] = weighted

    def near_block(slot):
        there = frame - core - 4 + slot
        hits = jnp.int32(0)
        for j in range(slots):
            hits += jnp.where((lists[0, j] == there) & (j < counts[0]), 1, 0)
        penalty = jnp.where(hits > 0, jnp.float32(0), jnp.float32(FAR))
        return k_near.at[slot], v_near.at[slot], penalty

    def absorb_near(w, *which):
        absorb(w, [near_block(slot) for slot in which])

    first_axis, first_at = (x, x, y, y), (at_x, at_x, at_y, at_y)
    second_axis, second_at = (y, y, x, x), (at_y, at_y, at_x, at_x)
    order = (1, 3, 2)
    mine = jnp.where(owner[0] == frame, 1.0, 0.0).astype(jnp.bfloat16)
    theirs = jnp.where(owner[0] == frame + 1 - 2 * core, 1.0, 0.0).astype(jnp.bfloat16)
    carried = style.at[core]

    def block_rows(s, j):
        return pl.ds(pl.multiple_of(base[s] + lax.rem(first_axis[s] + j, 4) * block[s], bit[s]), block[s])

    def bit_rows(s, j):
        return pl.ds(pl.multiple_of(lax.rem(second_axis[s] + j, 4) * bit[s], bit[s]), bit[s])

    def place_of(s, j):
        first = s - s % 2
        return base[first] + lax.rem(first_axis[s] + j, 4) * (2 * block[s]) + s % 2 * block[s]

    def place(s, j):
        return pl.ds(pl.multiple_of(place_of(s, j), block[s]), block[s])

    def own_bit(s):
        return pl.ds(pl.multiple_of(place_of(s, 0) + second_axis[s] * bit[s], bit[s]), bit[s])

    whole_block = tuple(pl.ds(0, n) for n in block)
    whole_bit = tuple(pl.ds(0, n) for n in bit)
    chosen, narrowed, settled, widened, shown = {}, {}, {}, {}, {}

    def choose(s, w):
        c, r = cols[w], half_rows(s)
        if w == 0:
            keep(s, 0).wait()
        given[s, w].wait_recv()
        ref_sel[r, c] = ref_own[r, c] * mine + ref_sib[r, c] * theirs
        chosen[s, w] = [
            send(ref_sel.at[block_rows(s, j), c], x_parts.at[s, j - 1, whole_block[s], c], first_at[s](j)) for j in order
        ]

    def narrow(s, w):
        c = cols[w]
        for copy in chosen[s, w]:
            copy.wait_recv()
        b = whole_block[s]
        x_sum[s, b, c] = (
            ref_sel[block_rows(s, 0), c] + x_parts[s, 0, b, c] + x_parts[s, 1, b, c] + x_parts[s, 2, b, c]
        )
        narrowed[s, w] = [
            send(x_sum.at[s, bit_rows(s, j), c], y_parts.at[s, j - 1, whole_bit[s], c], second_at[s](j)) for j in order
        ]

    def settle(s, w):
        c = cols[w]
        for copy in narrowed[s, w]:
            copy.wait_recv()
        b = whole_bit[s]
        carried[own_bit(s), c] = (
            x_sum[s, bit_rows(s, 0), c] + y_parts[s, 0, b, c] + y_parts[s, 1, b, c] + y_parts[s, 2, b, c]
        )
        here = carried.at[own_bit(s), c]
        settled[s, w] = [send(here, here, second_at[s](j)) for j in order]

    def widen(s, w):
        for copy in settled[s, w]:
            copy.wait_recv()
        here = carried.at[place(s, 0), cols[w]]
        widened[s, w] = {j: send(here, here, first_at[s](j)) for j in order}
        shown[s, w, 0] = send(here, here, sibling)

    def show(s, w, j):
        widened[s, w][j].wait_recv()
        there = carried.at[place(s, 4 - j), cols[w]]
        shown[s, w, j] = send(there, there, sibling)

    def absorb_style(w, j):
        for s in range(chains):
            shown[s, w, j].wait_recv()
        blocks = []
        for s in range(0, chains, 2):
            rows_of = pl.ds(pl.multiple_of(place_of(s, 4 - j), 2 * block[s]), 2 * block[s])
            blocks.append((style.at[0, rows_of], style.at[1, rows_of], None))
        absorb(w, blocks)

    def both(stage, which):
        for s in which:
            stage(s, 0)

    def finish(w):
        for h in heads[w]:
            att[:, pl.ds(h * HD, HD)] = (acc[h] / total[h]).T.astype(jnp.bfloat16)

    parts = width // LANES
    signs = (1, -1)
    whole = pl.ds(0, rows)

    def share(o, some):
        return dot(att[some, cols[0]], w_sum[:, column_block(o)], ((1,), (0,)))

    def hop(way, step, part):
        i = (step * 2 + way) * parts + part
        some = pl.ds(way * half, half) if step == 0 else whole
        return pltpu.make_async_remote_copy(
            src_ref=z_out.at[step, way, part, some], dst_ref=z_in.at[step, way, part, some],
            send_sem=z_send.at[i], recv_sem=z_recv.at[i],
            device_id=at_z(signs[way]), device_id_type=MESH,
        )

    def climb(step):
        some = [pl.ds(way * half, half) if step == 0 else whole for way in (0, 1)]
        shares = [share(signs[way] * (4 - step), some[way]) for way in (0, 1)]
        for part in range(parts):
            for way in (0, 1):
                value = shares[way][:, part * LANES : (part + 1) * LANES]
                if step == 0:
                    z_out[step, way, part, some[way]] = value.astype(jnp.bfloat16)
                elif step == 1:
                    hop(way, 0, part).wait_recv()
                    for which in (0, 1):
                        here = pl.ds(which * half, half)
                        one = value[which * half : (which + 1) * half]
                        if which == way:
                            one = one + z_in[0, way, part, here].astype(jnp.float32)
                        z_out[step, way, part, here] = one.astype(jnp.bfloat16)
                else:
                    hop(way, step - 1, part).wait_recv()
                    z_out[step, way, part] = (value + z_in[step - 1, way, part].astype(jnp.float32)).astype(
                        jnp.bfloat16
                    )
                hop(way, step, part).start()

    def drain(steps):
        for step in steps:
            for way in (0, 1):
                for part in range(parts):
                    hop(way, step, part).wait_send()

    both(choose, sooner)
    get_q.wait()
    get_k.wait()
    get_v.wait()
    absorb(0, [(k_near.at[own], v_near.at[own], None)])
    both(choose, later)
    to_next(0, v_hbm, v_near)
    for copy in to_sib:
        copy.wait_recv()
    absorb_near(0, 5 - core)
    both(narrow, sooner)
    both(narrow, later)
    relay(0)
    absorb_near(0, slot_of(-1), slot_of(1))
    both(settle, sooner)
    both(settle, later)
    for copy in passed[0]:
        copy.wait_recv()
    absorb_near(0, 3 - core, 7 - core)
    both(widen, sooner)
    both(widen, later)
    relay_far(0)
    absorb_near(0, slot_of(-2), slot_of(2))
    for copy in gone[0]:
        copy.wait_recv()
    absorb_near(0, 1 + 7 * core)
    absorb_style(0, 0)
    for j in (1, 3):
        for s in sooner + later:
            show(s, 0, j)
    absorb_style(0, 1)
    for s in sooner + later:
        show(s, 0, 2)
    absorb_style(0, 3)
    absorb_style(0, 2)
    finish(0)
    get_w.wait()
    for step in range(4):
        climb(step)
        for copy in made[step::4]:
            copy.wait_send()
    mine_here = share(0, whole)
    drain(range(3))
    for part in range(parts):
        lanes = pl.ds(part * LANES, LANES)
        for way in (0, 1):
            hop(way, 3, part).wait_recv()
        value = mine_here[:, part * LANES : (part + 1) * LANES]
        for way in (0, 1):
            value = value + z_in[3, way, part].astype(jnp.float32)
        out_ref[:, lanes] = value.astype(out_ref.dtype)

    drain((3,))


def per_device(
    queries, key_rows, value_rows, ref_keys, ref_values, key_lists, list_counts, owner_index, out_weight, residual,
    gate_scale,
):
    rows, width = queries.shape
    heads = width // HD
    ref_rows = ref_keys.shape[1]
    block, bit = ref_rows // 16, ref_rows // 64
    bf16, f32 = jnp.bfloat16, jnp.float32
    hbm = pl.BlockSpec(memory_space=pl.ANY)
    vmem = pl.BlockSpec(memory_space=pltpu.VMEM)
    smem = pl.BlockSpec(memory_space=pltpu.SMEM)
    copies = 96
    hops = 4 * 2 * (width // LANES)
    projected = pl.pallas_call(
        kernel,
        out_shape=jax.ShapeDtypeStruct((rows, width), f32),
        in_specs=[hbm] * 5 + [smem] * 3 + [hbm],
        out_specs=vmem,
        scratch_shapes=[
            pltpu.VMEM((rows, width), bf16),
            pltpu.VMEM((10, rows, width), bf16),
            pltpu.VMEM((10, rows, width), bf16),
            pltpu.VMEM((ref_rows, width), bf16),
            pltpu.VMEM((ref_rows, width), bf16),
            pltpu.VMEM((ref_rows, width), bf16),
            pltpu.VMEM((4, 3, block, width), bf16),
            pltpu.VMEM((4, block, width), bf16),
            pltpu.VMEM((4, 3, bit, width), bf16),
            pltpu.VMEM((2, ref_rows, width), bf16),
            pltpu.VMEM(out_weight.shape, bf16),
            pltpu.VMEM((heads, 1, rows), f32),
            pltpu.VMEM((heads, 1, rows), f32),
            pltpu.VMEM((heads, HD, rows), f32),
            pltpu.VMEM((rows, width), bf16),
            pltpu.VMEM((4, 2, width // LANES, rows, LANES), bf16),
            pltpu.VMEM((4, 2, width // LANES, rows, LANES), bf16),
            pltpu.SemaphoreType.DMA((8,)),
            pltpu.SemaphoreType.DMA((copies,)),
            pltpu.SemaphoreType.DMA((copies,)),
            pltpu.SemaphoreType.DMA((hops,)),
            pltpu.SemaphoreType.DMA((hops,)),
        ],
        compiler_params=pltpu.CompilerParams(
            collective_id=0, has_side_effects=True, vmem_limit_bytes=60 * 1024 * 1024
        ),
        name="block",
    )(
        queries, key_rows, value_rows, ref_keys, ref_values, key_lists, list_counts, owner_index, out_weight,
    )
    return (residual.astype(f32) + gate_scale[None, :] * projected).astype(bf16)


def solution(mesh):
    placed = (
        P("frame", "head"),
        P("frame", "head"),
        P("frame", "head"),
        P("frame", None, "head"),
        P("frame", None, "head"),
        P("frame", None),
        P("frame"),
        P(),
        P("head", None),
        P("frame", "head"),
        P("head"),
    )
    return jax.shard_map(
        per_device, mesh=mesh, in_specs=placed, out_specs=P("frame", "head"), check_vma=False
    )
```
